32 devices in a mesh: dp: 2 (over x), ctx: 4 (over z), fsdp: 4 (over y, core).
Axes of the slice: x: 2, y: 2, z: 4, core: 2. Of those that a mesh axis runs over, the one named last changes fastest.
Arguments:
- tokens: bfloat16 [2, 4, 3072, 2048], P('dp', 'fsdp', 'ctx'), may hold values from -6 to 6
- cotangent: bfloat16 [2, 4, 3072, 2048], P('dp', 'fsdp', 'ctx'), may hold values from -6 to 6
- pairing: int32 [2, 4, 4], P('dp', 'fsdp'), may hold values from 0 to 3, each once within a row
- attention_weights: float32 [2048, 8192], P(('dp', 'ctx', 'fsdp')), may hold values from -0.125 to 0.125
- attention_moment: float32 [2048, 8192], P(('dp', 'ctx', 'fsdp')), may hold values from -112 to 112
- attention_square: float32 [2048, 8192], P(('dp', 'ctx', 'fsdp')), may hold values from 1302.528 to 5160.96
- feed_weights: float32 [2048, 24576], P(('dp', 'ctx', 'fsdp')), may hold values from -0.125 to 0.125
- feed_moment: float32 [2048, 24576], P(('dp', 'ctx', 'fsdp')), may hold values from -80 to 80
- feed_square: float32 [2048, 24576], P(('dp', 'ctx', 'fsdp')), may hold values from 638.976 to 2580.48
- gains: float32 [4, 2048], replicated, may hold values from 0.5 to 1.5
- gain_moment: float32 [4, 2048], replicated, may hold values from -112 to 112
- gain_square: float32 [4, 2048], replicated, may hold values from 1302.528 to 5160.96
Outputs:
- output_states: bfloat16 [2, 4, 3072, 2048], P('dp', 'fsdp', 'ctx')
- input_gradient: bfloat16 [2, 4, 3072, 2048], P('dp', 'fsdp', 'ctx')
- attention_gradient: float32 [2048, 8192], P(('dp', 'ctx', 'fsdp'))
- attention_moment_new: float32 [2048, 8192], P(('dp', 'ctx', 'fsdp'))
- attention_square_new: float32 [2048, 8192], P(('dp', 'ctx', 'fsdp'))
- attention_weights_new: float32 [2048, 8192], P(('dp', 'ctx', 'fsdp'))
- feed_gradient: float32 [2048, 24576], P(('dp', 'ctx', 'fsdp'))
- feed_moment_new: float32 [2048, 24576], P(('dp', 'ctx', 'fsdp'))
- feed_square_new: float32 [2048, 24576], P(('dp', 'ctx', 'fsdp'))
- feed_weights_new: float32 [2048, 24576], P(('dp', 'ctx', 'fsdp'))
- gain_gradient: float32 [4, 2048], replicated
- gain_moment_new: float32 [4, 2048], replicated
- gain_square_new: float32 [4, 2048], replicated
- gains_new: float32 [4, 2048], replicated
The draws below stay inside these ranges and needn't reach their ends.
Inputs may be any that keep to these rules, and one draw needn't show every extreme that they name: Each row of pairing is a permutation of 0 to 3.
All inputs are finite; a program needn't handle non-finite values.
Results may differ from the reference program's by a relative error of at most 0.018.
Values may be sent and summed in bfloat16 or wider, within the bound.
A program may use at most 896 MiB of HBM per device.

```python
import math
import jax
import jax.numpy as jnp
from jax import lax

D = 2048
HEADS = 16
HEAD = 128
FF = 8192
SEQ_LEN = 3072
STEP = 10
BLK = 384
TOKENS = 24576
N_DP = 2
N_CTX = 4
N_FSDP = 4


def shard_levels(rng, extent, shards, least, high):
    level = 1.0
    for position, parts in shards:
        steps = jax.random.uniform(jax.random.fold_in(jax.random.fold_in(rng, 6), position), (parts,), jnp.float32, least / len(shards), high / len(shards))
        level = level * jnp.repeat(jnp.exp(steps), extent[position] // parts).reshape((-1,) + (1,) * (len(extent) - 1 - position))
    return level


def centred(key, dims, spread, reach, cuts=(), kind=jnp.bfloat16):
    values = spread * jax.random.normal(key, dims, jnp.float32)
    if cuts:
        values = values * shard_levels(key, dims, cuts, -0.22, 0.18)
    return jnp.clip(values, -reach, reach).astype(kind)


def setup_inputs(seed: int = 0) -> dict:
    arg_keys = jax.random.split(jax.random.key(seed), 13)
    return {
        "tokens": centred(arg_keys[0], (N_DP, N_FSDP, SEQ_LEN, D), 1.0, 6.0, ((0, 2), (1, 4), (2, 4))),
        "cotangent": centred(arg_keys[1], (N_DP, N_FSDP, SEQ_LEN, D), 1.0, 6.0, ((0, 2), (1, 4), (2, 4))),
        "pairing": jax.vmap(lambda own: jax.random.permutation(own, N_CTX))(jax.random.split(arg_keys[2], N_DP * N_FSDP)).reshape((N_DP, N_FSDP, N_CTX)).astype(jnp.int32),
        "attention_weights": centred(arg_keys[3], (D, 4 * D), D ** -0.5, 0.125, ((0, 32),), jnp.float32),
        "attention_moment": centred(arg_keys[4], (D, 4 * D), (0.11 * TOKENS ** 0.5), 112.0, ((0, 32),), jnp.float32),
        "attention_square": jnp.clip(jnp.exp(math.log(5160.96) - 1.37681564 * jax.random.uniform(arg_keys[5], (D, 4 * D), jnp.float32) ** shard_levels(arg_keys[5], (D, 4 * D), ((0, 32),), -0.2, 0.2)), 1302.528, 5160.96),
        "feed_weights": centred(arg_keys[6], (D, 3 * FF), D ** -0.5, 0.125, ((0, 32),), jnp.float32),
        "feed_moment": centred(arg_keys[7], (D, 3 * FF), (0.08 * TOKENS ** 0.5), 80.0, ((0, 32),), jnp.float32),
        "feed_square": jnp.clip(jnp.exp(math.log(2580.48) - 1.3958638 * jax.random.uniform(arg_keys[8], (D, 3 * FF), jnp.float32) ** shard_levels(arg_keys[8], (D, 3 * FF), ((0, 32),), -0.2, 0.2)), 638.976, 2580.48),
        "gains": jnp.clip(1.0 + 0.1 * jax.random.normal(arg_keys[9], (4, D), jnp.float32), 0.5, 1.5),
        "gain_moment": centred(arg_keys[10], (4, D), (0.11 * TOKENS ** 0.5), 112.0, (), jnp.float32),
        "gain_square": jnp.clip(jnp.exp(jax.random.uniform(arg_keys[11], (4, D), jnp.float32, math.log(1302.528), math.log(5160.96))), 1302.528, 5160.96),
    }


epsilon_norm = 1e-06
rope_base = 500000.0
masked_value = -1e+30
beta_first = 0.9
beta_second = 0.95
learn_rate = 0.05
gain_rate = 1.0
weight_decay = 0.1
epsilon_adam = 1e-08

@jax.custom_vjp
def low(v):
    return lax.optimization_barrier(v.astype(jnp.bfloat16)).astype(jnp.float32)

@jax.custom_vjp
def low_back(v):
    return v

def low_keep(v):
    return (low(v), None)

def low_pass(kept, grad):
    return (grad,)

def back_keep(v):
    return (v, None)

def back_low(kept, grad):
    return (low(grad),)
low.defvjp(low_keep, low_pass)
low_back.defvjp(back_keep, back_low)

def stored_positions(pair_row, length, block, ctx_count):
    index = jnp.arange(length, dtype=jnp.int32)
    owner = index // (2 * block)
    upper = index // block % 2
    table = lax.optimization_barrier(jnp.sum(jnp.where(owner[:, None] == jnp.arange(ctx_count, dtype=jnp.int32)[None, :], pair_row[None, :], 0), axis=1)).astype(jnp.int32)
    placed = jnp.where(upper == 0, table, 2 * ctx_count - 1 - table)
    return (placed * block + index % block).astype(jnp.int32)

def rotate(values, places, sign):
    rows = values.shape[0]
    half = HEAD // 2
    frequency = rope_base ** (-(jnp.arange(half, dtype=jnp.float32) * (2.0 / HEAD)))
    angle = places.astype(jnp.float32)[:, None] * frequency[None, :]
    cosine = jnp.cos(angle)[:, None, :]
    sine = sign * jnp.sin(angle)[:, None, :]
    shaped = values.reshape(rows, HEADS, HEAD)
    first = shaped[..., :half]
    second = shaped[..., half:]
    turned = jnp.concatenate([first * cosine - second * sine, second * cosine + first * sine], axis=-1)
    return turned.reshape(rows, HEADS * HEAD)

def norm_apply(values, gain):
    return values * lax.rsqrt(lax.optimization_barrier(jnp.mean(values * values, axis=-1, keepdims=True)) + epsilon_norm) * gain

def product(left, right):
    return jnp.dot(left, right, precision=lax.Precision.HIGHEST, preferred_element_type=jnp.float32)

def product_against(left, right):
    return lax.dot_general(left, right, (((1,), (1,)), ((), ())), precision=lax.Precision.HIGHEST, preferred_element_type=jnp.float32)

def attention(queries, keys, values, places):
    length = queries.shape[0]
    block = 512 if length % 512 == 0 else length
    scale = HEAD ** (-0.5)
    key_heads = keys.reshape(length, HEADS, HEAD)
    value_heads = values.reshape(length, HEADS, HEAD)
    query_blocks = queries.reshape(length // block, block, HEADS, HEAD)
    place_blocks = places.reshape(length // block, block)

    def one_block(pieces):
        query_piece, place_piece = pieces
        scores = low_back(jnp.einsum('qhd,khd->hqk', query_piece, key_heads, precision=lax.Precision.HIGHEST) * scale)
        allowed = places[None, None, :] <= place_piece[None, :, None]
        masked = jnp.where(allowed, scores, masked_value)
        log_total = jax.nn.logsumexp(masked, axis=-1, keepdims=True)
        weights = low(jnp.where(allowed, jnp.exp(masked - log_total), 0.0))
        mixed = jnp.einsum('hqk,khd->qhd', weights, value_heads, precision=lax.Precision.HIGHEST)
        return mixed.reshape(block, HEADS * HEAD)
    return lax.map(jax.checkpoint(one_block), (query_blocks, place_blocks)).reshape(length, HEADS * HEAD)

def sequence_layer(inputs, places, attention_low, feed_low, gains):
    width = inputs.shape[1]
    hidden = feed_low.shape[1] // 3
    query_pre = low_back(product(inputs, attention_low[:, :width]))
    key_pre = low_back(product(inputs, attention_low[:, width:2 * width]))
    values = low(low_back(product(inputs, attention_low[:, 2 * width:3 * width])))
    queries = low(rotate(norm_apply(query_pre, gains[0]), places, 1.0))
    keys = low(rotate(norm_apply(key_pre, gains[1]), places, 1.0))
    attended = low(low_back(attention(queries, keys, values, places)))
    proj = low_back(product(attended, attention_low[:, 3 * width:]))
    state = inputs + norm_apply(proj, gains[2])
    state_low = low(state)
    gate = low_back(product(state_low, feed_low[:, :hidden]))
    up = low_back(product(state_low, feed_low[:, hidden:2 * hidden]))
    inner = low(jax.nn.silu(gate) * up)
    down = low_back(product_against(inner, feed_low[:, 2 * hidden:]))
    return state + norm_apply(down, gains[3])

def adamw(weight, moment, square, gradient, rate, decay):
    moment_new = beta_first * moment + (1.0 - beta_first) * gradient
    square_new = beta_second * square + (1.0 - beta_second) * gradient * gradient
    fix_first = 1.0 - beta_first ** STEP
    fix_second = 1.0 - beta_second ** STEP
    update = moment_new / fix_first / (jnp.sqrt(square_new / fix_second) + epsilon_adam)
    return (moment_new, square_new, weight - rate * (update + decay * weight))

def reference(tokens, cotangent, pairing, attention_weights, attention_moment, attention_square, feed_weights, feed_moment, feed_square, gains, gain_moment, gain_square):
    groups = N_DP * N_FSDP
    flat = tokens.astype(jnp.float32).reshape(groups, SEQ_LEN, D)

    def sequence_places(pair_row):
        return stored_positions(pair_row, SEQ_LEN, BLK, N_CTX)
    places = jax.vmap(sequence_places)(pairing.reshape(groups, N_CTX))

    def forward(flat_in, attention_in, feed_in, gain_in):
        attention_low = low(attention_in)
        feed_low = low(feed_in)

        def one_sequence(pieces):
            return sequence_layer(pieces[0], pieces[1], attention_low, feed_low, gain_in)
        return lax.map(jax.checkpoint(one_sequence), (flat_in, places))
    result, pullback = jax.vjp(forward, flat, attention_weights, feed_weights, gains)
    grad_flat, grad_attention, grad_feed, grad_gain = pullback(cotangent.astype(jnp.float32).reshape(groups, SEQ_LEN, D))
    attention_moment_new, attention_square_new, attention_weights_new = adamw(attention_weights, attention_moment, attention_square, grad_attention, learn_rate, weight_decay)
    feed_moment_new, feed_square_new, feed_weights_new = adamw(feed_weights, feed_moment, feed_square, grad_feed, learn_rate, weight_decay)
    gain_moment_new, gain_square_new, gains_new = adamw(gains, gain_moment, gain_square, grad_gain, gain_rate, 0.0)
    output_states = result.astype(jnp.bfloat16).reshape(tokens.shape)
    input_gradient = grad_flat.astype(jnp.bfloat16).reshape(tokens.shape)
    return (output_states, input_gradient, grad_attention, attention_moment_new, attention_square_new, attention_weights_new, grad_feed, feed_moment_new, feed_square_new, feed_weights_new, grad_gain, gain_moment_new, gain_square_new, gains_new)
```

```python
import functools
import math

import jax
import jax.numpy as jnp
from jax import lax
from jax.experimental import pallas as pl
from jax.experimental.pallas import tpu as pltpu
from jax.sharding import PartitionSpec as P

HEADS = 16
HEAD = 128
STEP = 10

epsilon_norm = 1e-06
rope_base = 500000.0
masked_value = -1e30
beta_first = 0.9
beta_second = 0.95
learn_rate = 0.05
gain_rate = 1.0
weight_decay = 0.1
epsilon_adam = 1e-08

score_scale = HEAD ** (-0.5)
exponent_scale = score_scale * math.log2(math.e)

EVERY = ("dp", "ctx", "fsdp")


def turn_tables(places):
    half = HEAD // 2
    frequency = rope_base ** (-(jnp.arange(half, dtype=jnp.float32) * (2.0 / HEAD)))
    angle = places.astype(jnp.float32)[:, None] * frequency[None, :]
    cosine = jnp.cos(angle)
    sine = jnp.sin(angle)
    return (
        jnp.concatenate([cosine, cosine], axis=-1),
        jnp.concatenate([-sine, sine], axis=-1),
    )


def norm_backward(values, scale, gain, upstream):
    weighted = upstream * gain
    inward = scale * (
        weighted - values * (scale * scale) * jnp.mean(weighted * values, axis=-1, keepdims=True)
    )
    return inward, jnp.sum(upstream * values * scale, axis=0)


def product(left, right):
    return jnp.dot(left, right, preferred_element_type=jnp.float32)


def transposed(left, right):
    return lax.dot_general(
        left, right, (((0,), (0,)), ((), ())), preferred_element_type=jnp.float32
    )


def against(left, right):
    return lax.dot_general(
        left, right, (((1,), (1,)), ((), ())), preferred_element_type=jnp.float32
    )


low_type = jnp.bfloat16


def tile_of(length):
    for tile in (512, 384, 256, 128):
        if length % tile == 0:
            return tile
    return length


brief = pl.CostEstimate(flops=1024, bytes_accessed=1024, transcendentals=0)


def params(steps, mib):
    return pltpu.CompilerParams(
        dimension_semantics=("arbitrary",) * steps, vmem_limit_bytes=mib * 2**20
    )


def prepare_kernel(order_ref, q_ref, k_ref, v_ref, scale_ref, gain_ref, cos_ref, sin_ref, qo, ko, vo):
    cosine, sine = cos_ref[...], sin_ref[...]
    for which, (source, target) in enumerate(((q_ref, qo), (k_ref, ko))):
        scale = scale_ref[:, which : which + 1]
        for start in range(0, source.shape[1], HEAD):
            at = slice(start, start + HEAD)
            part = source[:, at] * scale * gain_ref[which : which + 1, at]
            turned = part * cosine + pltpu.roll(part, HEAD // 2, 1) * sine
            target[:, at] = turned.astype(low_type)
    vo[...] = v_ref[...].astype(low_type)


def prepare(projected, scales, gains, cosine, sine, order, stream):
    length, width = projected.shape[0] // 2, projected.shape[1] // 3
    count = order.shape[0]
    block = length // count
    out = pl.BlockSpec((block, width), lambda b, o: (o[b], 0))
    turn = pl.BlockSpec((block, HEAD), lambda b, o: (o[b], 0))
    return pl.pallas_call(
        prepare_kernel,
        out_shape=(jax.ShapeDtypeStruct((length, width), low_type),) * 3,
        grid_spec=pltpu.PrefetchScalarGridSpec(
            num_scalar_prefetch=1,
            grid=(count,),
            in_specs=[
                pl.BlockSpec((block, width), lambda b, o: (2 * b + stream, 0)),
                pl.BlockSpec((block, width), lambda b, o: (2 * b + stream, 1)),
                pl.BlockSpec((block, width), lambda b, o: (2 * b + stream, 2)),
                pl.BlockSpec((block, 2), lambda b, o: (2 * b + stream, 0)),
                pl.BlockSpec((2, width), lambda b, o: (0, 0)),
                turn,
                turn,
            ],
            out_specs=(out, out, out),
        ),
        compiler_params=params(1, 32),
        cost_estimate=brief,
        name="prepare",
    )(order, projected, projected, projected, scales, gains, cosine, sine)


def restore_kernel(
    order_ref,
    dq_ref,
    dk_ref,
    dv_ref,
    q_ref,
    k_ref,
    scale_ref,
    gain_ref,
    cos_ref,
    sin_ref,
    out_ref,
    value_ref,
    dot_ref,
    sum_ref,
):
    cosine, sine = cos_ref[...] * score_scale, sin_ref[...] * score_scale
    width = q_ref.shape[1]

    @pl.when(pl.program_id(0) == 0)
    def _():
        sum_ref[...] = jnp.zeros_like(sum_ref)

    for which, (source, pre) in enumerate(((dq_ref, q_ref), (dk_ref, k_ref))):
        scale = scale_ref[:, which : which + 1]
        dots = 0.0
        for start in range(0, width, HEAD):
            at = slice(start, start + HEAD)
            part = source[:, at]
            turned = part * cosine - pltpu.roll(part, HEAD // 2, 1) * sine
            weighted = turned * gain_ref[which : which + 1, at]
            unit = pre[:, at] * scale
            out_ref[:, which * width + start : which * width + start + HEAD] = weighted
            dots = dots + jnp.sum(weighted * unit, axis=1, keepdims=True)
            sum_ref[which : which + 1, at] += jnp.sum(turned * unit, axis=0, keepdims=True)
        dot_ref[:, which : which + 1] = dots
    value_ref[...] = dv_ref[...].astype(low_type)


def restore(grads, projected, scales, gains, cosine, sine, order, stream):
    length, width = grads[0].shape
    count = order.shape[0]
    block = length // count
    first = stream * count
    later = pl.BlockSpec((block, width), lambda b, o: (first + o[b], 0))
    turn = pl.BlockSpec((block, HEAD), lambda b, o: (o[b], 0))
    both = pl.BlockSpec((block, 2), lambda b, o: (b, 0))
    scale = pl.BlockSpec((block, 2), lambda b, o: (2 * b + stream, 0))
    small = pl.BlockSpec((2, width), lambda b, o: (0, 0))
    return pl.pallas_call(
        restore_kernel,
        out_shape=(
            jax.ShapeDtypeStruct((length, 2 * width), jnp.float32),
            jax.ShapeDtypeStruct((length, width), low_type),
            jax.ShapeDtypeStruct((length, 2), jnp.float32),
            jax.ShapeDtypeStruct((2, width), jnp.float32),
        ),
        grid_spec=pltpu.PrefetchScalarGridSpec(
            num_scalar_prefetch=1,
            grid=(count,),
            in_specs=[
                pl.BlockSpec((block, width), lambda b, o: (o[b], 0)),
                later,
                later,
                pl.BlockSpec((block, width), lambda b, o: (2 * b + stream, 0)),
                pl.BlockSpec((block, width), lambda b, o: (2 * b + stream, 1)),
                scale,
                small,
                turn,
                turn,
            ],
            out_specs=(
                pl.BlockSpec((block, 2 * width), lambda b, o: (b, 0)),
                pl.BlockSpec((block, width), lambda b, o: (b, 0)),
                both,
                small,
            ),
        ),
        compiler_params=params(1, 40),
        cost_estimate=brief,
        name="restore",
    )(order, *grads, projected, projected, scales, gains, cosine, sine)


def causal(tile):
    key = lax.broadcasted_iota(jnp.int32, (tile, tile), 0)
    query = lax.broadcasted_iota(jnp.int32, (tile, tile), 1)
    return key <= query


def forward_kernel(tile, parts, spots_ref, q_ref, *refs):
    k_refs, v_refs = refs[:parts], refs[parts : 2 * parts]
    o_ref, log_ref, ks, vt, held_rows = refs[2 * parts :]
    rows = k_refs[0].shape[0]
    step = pl.program_id(1)

    @pl.when(step == 0)
    def _():
        for part in range(parts):
            ks[part * rows : (part + 1) * rows, :] = k_refs[part][...]
            for start in range(0, rows, tile):
                at = slice(part * rows + start, part * rows + start + tile)
                value = v_refs[part][start : start + tile, :]
                vt[:, at] = value.astype(jnp.float32).T.astype(low_type)

    query = q_ref[...]

    def visit(j, carry, masked):
        top, mass, held = carry
        at = pl.ds(pl.multiple_of(j * tile, tile), tile)
        scores = against(ks[at, :], query)
        if masked:
            scores = jnp.where(causal(tile), scores, masked_value)
        new_top = jnp.maximum(top, jnp.max(scores, axis=0, keepdims=True))
        weights = jnp.exp2((scores - new_top) * exponent_scale)
        fade = jnp.exp2((top - new_top) * exponent_scale)
        mass = mass * fade + jnp.sum(weights, axis=0, keepdims=True)
        held = held * fade + product(vt[:, at], weights.astype(low_type))
        return new_top, mass, held

    start = (
        jnp.full((1, tile), masked_value, jnp.float32),
        jnp.zeros((1, tile), jnp.float32),
        jnp.zeros((HEAD, tile), jnp.float32),
    )
    last = step + (parts - 1) * (rows // tile)
    carry = visit(last, start, True)
    top, mass, held = lax.fori_loop(0, last, lambda j, c: visit(j, c, False), carry)
    here = pl.ds(pl.multiple_of(step * tile, tile), tile)
    held_rows[here, :] = (held / mass).T.astype(low_type)
    log_ref[0] = top * exponent_scale + jnp.log2(mass)

    @pl.when(step == rows // tile - 1)
    def _():
        count = spots_ref.shape[0]
        block = rows // count
        for k in range(count):
            there = pl.ds(pl.multiple_of(spots_ref[k] * block, block), block)
            o_ref[k * block : (k + 1) * block, :] = held_rows[there, :]


def attend_forward(queries, keys, values, spots):
    length, width = queries.shape
    heads, parts = width // HEAD, len(keys)
    tile = tile_of(length)
    whole = pl.BlockSpec((length, HEAD), lambda h, i, o: (0, h))
    piece = pl.BlockSpec((tile, HEAD), lambda h, i, o: (i, h))
    return pl.pallas_call(
        functools.partial(forward_kernel, tile, parts),
        out_shape=(
            jax.ShapeDtypeStruct((length, width), low_type),
            jax.ShapeDtypeStruct((heads, 1, length), jnp.float32),
        ),
        grid_spec=pltpu.PrefetchScalarGridSpec(
            num_scalar_prefetch=1,
            grid=(heads, length // tile),
            in_specs=[piece] + [whole] * (2 * parts),
            out_specs=(whole, pl.BlockSpec((1, 1, tile), lambda h, i, o: (h, 0, i))),
            scratch_shapes=[
                pltpu.VMEM((parts * length, HEAD), low_type),
                pltpu.VMEM((HEAD, parts * length), low_type),
                pltpu.VMEM((length, HEAD), low_type),
            ],
        ),
        compiler_params=params(2, 40),
        cost_estimate=brief,
        name="attend_forward",
    )(spots, queries, *keys, *values)


def backward_kernel(tile, parts, extra, spots_ref, q_ref, g_ref, o_ref, log_ref, *refs):
    k_refs, v_refs = refs[:parts], refs[parts : 2 * parts]
    added = refs[2 * parts : 2 * parts + extra]
    dq_ref, dk_ref, dv_ref, ks, vs, kt, gs, os, delta, dqt = refs[2 * parts + extra :]
    rows = q_ref.shape[0]
    steps = rows // tile
    step = pl.program_id(1)

    @pl.when(step == 0)
    def _():
        for part in range(parts):
            ks[part * rows : (part + 1) * rows, :] = k_refs[part][...]
            vs[part * rows : (part + 1) * rows, :] = v_refs[part][...]
            for start in range(0, rows, tile):
                at = slice(part * rows + start, part * rows + start + tile)
                key = k_refs[part][start : start + tile, :]
                kt[:, at] = key.astype(jnp.float32).T.astype(low_type)
        count = spots_ref.shape[0]
        block = rows // count
        for k in range(count):
            there = pl.ds(pl.multiple_of(spots_ref[k] * block, block), block)
            gs[there, :] = g_ref[k * block : (k + 1) * block, :]
            os[there, :] = o_ref[k * block : (k + 1) * block, :]
        for start in range(0, rows, tile):
            at = slice(start, start + tile)
            both = gs[at, :].astype(jnp.float32) * os[at, :].astype(jnp.float32)
            delta[:, at] = jnp.sum(both.T, axis=0, keepdims=True)
        dqt[...] = jnp.zeros_like(dqt)

    here = pl.ds(pl.multiple_of(step * tile, tile), tile)
    key, value, key_turned = ks[here, :], vs[here, :], kt[:, here]

    def visit(i, carry, masked):
        key_sum, value_sum = carry
        at = pl.ds(pl.multiple_of(i * tile, tile), tile)
        query, outward = q_ref[at, :], gs[at, :]
        scores = against(key, query)
        exact = jnp.exp2(scores * exponent_scale - log_ref[0, :, at])
        if masked:
            exact = jnp.where(causal(tile), exact, 0.0)
        slope = (exact * (against(value, outward) - delta[:, at])).astype(low_type)
        value_sum = value_sum + product(exact.astype(low_type), outward)
        key_sum = key_sum + product(slope, query)
        dqt[:, at] += product(key_turned, slope)
        return key_sum, value_sum

    if extra:
        carry = (added[0][...], added[1][...])
    else:
        carry = (jnp.zeros((tile, HEAD), jnp.float32),) * 2
    own = step - (parts - 1) * steps

    def store(carry):
        dk_ref[...], dv_ref[...] = carry

    @pl.when(own < 0)
    def _():
        store(lax.fori_loop(0, steps, lambda i, c: visit(i, c, False), carry))

    @pl.when(own >= 0)
    def _():
        first = visit(own, carry, True)
        store(lax.fori_loop(own + 1, steps, lambda i, c: visit(i, c, False), first))

    @pl.when(own == steps - 1)
    def _():
        for start in range(0, rows, tile):
            at = slice(start, start + tile)
            dq_ref[at, :] = dqt[:, at].T


def attend_backward(queries, outward, attended, logs, keys, values, added, spots):
    length, width = queries.shape
    heads, parts = width // HEAD, len(keys)
    tile = tile_of(length)
    whole = pl.BlockSpec((length, HEAD), lambda h, j, o: (0, h))
    piece = pl.BlockSpec((tile, HEAD), lambda h, j, o: (j, h))
    total = parts * length
    return pl.pallas_call(
        functools.partial(backward_kernel, tile, parts, len(added)),
        out_shape=(
            jax.ShapeDtypeStruct((length, width), jnp.float32),
            jax.ShapeDtypeStruct((total, width), jnp.float32),
            jax.ShapeDtypeStruct((total, width), jnp.float32),
        ),
        grid_spec=pltpu.PrefetchScalarGridSpec(
            num_scalar_prefetch=1,
            grid=(heads, total // tile),
            in_specs=[whole] * 3
            + [pl.BlockSpec((1, 1, length), lambda h, j, o: (h, 0, 0))]
            + [whole] * (2 * parts)
            + [piece] * len(added),
            out_specs=(whole, piece, piece),
            scratch_shapes=[
                pltpu.VMEM((total, HEAD), low_type),
                pltpu.VMEM((total, HEAD), low_type),
                pltpu.VMEM((HEAD, total), low_type),
                pltpu.VMEM((length, HEAD), low_type),
                pltpu.VMEM((length, HEAD), low_type),
                pltpu.VMEM((1, length), jnp.float32),
                pltpu.VMEM((HEAD, length), jnp.float32),
            ],
        ),
        compiler_params=params(2, 48),
        cost_estimate=brief,
        name="attend_backward",
    )(spots, queries, outward, attended, logs, *keys, *values, *added)


def out_kernel(others_ref, x_ref, w_ref, out_ref):
    @pl.when(pl.program_id(1) == 0)
    def _():
        out_ref[...] = jnp.zeros_like(out_ref)

    out_ref[...] += product(x_ref[0], w_ref[...])


def out_project(pieces, weight, others):
    count, rows, depth = pieces.shape
    width = weight.shape[1]
    across = min(1024, width)
    return pl.pallas_call(
        out_kernel,
        out_shape=jax.ShapeDtypeStruct((rows, width), jnp.float32),
        grid_spec=pltpu.PrefetchScalarGridSpec(
            num_scalar_prefetch=1,
            grid=(width // across, count),
            in_specs=[
                pl.BlockSpec((1, rows, depth), lambda n, k, o: (k, 0, 0)),
                pl.BlockSpec((depth, across), lambda n, k, o: (o[k], n)),
            ],
            out_specs=pl.BlockSpec((rows, across), lambda n, k, o: (0, n)),
        ),
        compiler_params=params(2, 32),
        cost_estimate=brief,
        name="out_project",
    )(others, pieces, weight)


def out_back_kernel(others_ref, x_ref, w_ref, out_ref):
    out_ref[0] = against(x_ref[...], w_ref[...]).astype(low_type)


def out_back(grad, weight, others):
    rows, width = grad.shape
    count = others.shape[0]
    depth = weight.shape[0] // count
    return pl.pallas_call(
        out_back_kernel,
        out_shape=jax.ShapeDtypeStruct((count, rows, depth), low_type),
        grid_spec=pltpu.PrefetchScalarGridSpec(
            num_scalar_prefetch=1,
            grid=(count,),
            in_specs=[
                pl.BlockSpec((rows, width), lambda k, o: (0, 0)),
                pl.BlockSpec((depth, width), lambda k, o: (o[k], 0)),
            ],
            out_specs=pl.BlockSpec((1, rows, depth), lambda k, o: (k, 0, 0)),
        ),
        compiler_params=params(1, 32),
        cost_estimate=brief,
        name="out_back",
    )(others, grad, weight)


def out_weight_kernel(streams, others_ref, *refs):
    lefts, rights, out_ref = refs[:streams], refs[streams:-1], refs[-1]
    total = 0.0
    for left, right in zip(lefts, rights):
        total = total + product(left[0].T, right[...])
    out_ref[...] = total.astype(low_type)


def out_weight(lefts, rights, others):
    count, rows, depth = lefts[0].shape
    width = rights[0].shape[1]
    across = min(1024, width)
    return pl.pallas_call(
        functools.partial(out_weight_kernel, len(lefts)),
        out_shape=jax.ShapeDtypeStruct((count * depth, width), low_type),
        grid_spec=pltpu.PrefetchScalarGridSpec(
            num_scalar_prefetch=1,
            grid=(width // across, count),
            in_specs=[pl.BlockSpec((1, rows, depth), lambda n, k, o: (k, 0, 0))] * len(lefts)
            + [pl.BlockSpec((rows, across), lambda n, k, o: (0, n))] * len(rights),
            out_specs=pl.BlockSpec((depth, across), lambda n, k, o: (o[k], n)),
        ),
        compiler_params=params(2, 32),
        cost_estimate=brief,
        name="out_weight",
    )(others, *lefts, *rights)


def chosen(refs, index, use):
    for i, ref in enumerate(refs):
        pl.when(index == i)(functools.partial(use, ref))


def gate_up_kernel(count, parts, *refs):
    pieces, refs = refs[:count], refs[count:]
    gates, ups = refs[:parts], refs[parts : 2 * parts]
    gate_ref, up_ref, inner_ref = refs[2 * parts :]
    half = pieces[0].shape[1] // parts

    def use(x_ref):
        gate = up = 0.0
        for p in range(parts):
            piece = x_ref[:, p * half : (p + 1) * half]
            gate = gate + product(piece, gates[p][...])
            up = up + product(piece, ups[p][...])
        gate_ref[...] = gate.astype(low_type)
        up_ref[...] = up.astype(low_type)
        inner_ref[...] = (gate * jax.nn.sigmoid(gate) * up).astype(low_type)

    chosen(pieces, pl.program_id(1), use)


def gate_up(pieces, gates, ups):
    count, (rows, width) = len(pieces), pieces[0].shape
    parts, columns = len(gates), gates[0].shape[1]
    across = min(512, columns)
    weight = pl.BlockSpec((width // parts, across), lambda n, m: (0, n))
    out = pl.BlockSpec((rows, across), lambda n, m: (m, n))
    return pl.pallas_call(
        functools.partial(gate_up_kernel, count, parts),
        grid=(columns // across, count),
        out_shape=(jax.ShapeDtypeStruct((count * rows, columns), low_type),) * 3,
        in_specs=[pl.BlockSpec((rows, width), lambda n, m: (0, 0))] * count
        + [weight] * (2 * parts),
        out_specs=(out,) * 3,
        compiler_params=params(2, 52),
        cost_estimate=brief,
        name="gate_up",
    )(*pieces, *gates, *ups)


def spread_kernel(terms, parts, *refs):
    lefts, weights, out = refs[:terms], refs[terms:-1], refs[-1]
    for p in range(parts):
        total = 0.0
        for t in range(terms):
            total = total + against(lefts[t][...], weights[t * parts + p][...])
        out[p] = total.astype(low_type)


def spread(lefts, weights, half):
    rows, columns = lefts[0].shape[0] // 2, lefts[0].shape[1]
    terms, parts, features = len(lefts), len(weights[0]), weights[0][0].shape[0]
    across = min(256, features)
    return pl.pallas_call(
        functools.partial(spread_kernel, terms, parts),
        grid=(features // across,),
        out_shape=jax.ShapeDtypeStruct((parts, rows, features), low_type),
        in_specs=[pl.BlockSpec((rows, columns), lambda n: (half, 0))] * terms
        + [pl.BlockSpec((across, columns), lambda n: (n, 0))] * (terms * parts),
        out_specs=pl.BlockSpec((parts, rows, across), lambda n: (0, 0, n)),
        compiler_params=params(1, 52),
        cost_estimate=brief,
        name="spread",
    )(*lefts, *[w for group in weights for w in group])


def inner_kernel(count, parts, *refs):
    pieces, (gate_ref, up_ref), refs = refs[:count], refs[count : count + 2], refs[count + 2 :]
    weights, (dgate_ref, dup_ref) = refs[:parts], refs[parts:]
    half = pieces[0].shape[1] // parts

    def use(x_ref):
        grad = 0.0
        for p in range(parts):
            grad = grad + product(x_ref[:, p * half : (p + 1) * half], weights[p][...])
        gate, up = gate_ref[...].astype(jnp.float32), up_ref[...].astype(jnp.float32)
        sigma = jax.nn.sigmoid(gate)
        dgate_ref[...] = (grad * up * sigma * (1.0 + gate * (1.0 - sigma))).astype(low_type)
        dup_ref[...] = (grad * gate * sigma).astype(low_type)

    chosen(pieces, pl.program_id(1), use)


def inner_backward(pieces, gate, up, downs):
    count, (rows, width) = len(pieces), pieces[0].shape
    parts, columns = len(downs), downs[0].shape[1]
    across = min(1024, columns)
    out = pl.BlockSpec((rows, across), lambda n, m: (m, n))
    return pl.pallas_call(
        functools.partial(inner_kernel, count, parts),
        grid=(columns // across, count),
        out_shape=(jax.ShapeDtypeStruct((count * rows, columns), low_type),) * 2,
        in_specs=[pl.BlockSpec((rows, width), lambda n, m: (0, 0))] * count
        + [out, out]
        + [pl.BlockSpec((width // parts, across), lambda n, m: (0, n))] * parts,
        out_specs=(out,) * 2,
        compiler_params=params(2, 52),
        cost_estimate=brief,
        name="inner_backward",
    )(*pieces, gate, up, *downs)


def weight_kernel(count, each, *refs):
    lefts, rights, (out, turned) = refs[:count], refs[count : count + count // each], refs[-2:]
    rows = lefts[0].shape[0]

    @pl.when(pl.program_id(1) == 0)
    def _():
        for c in range(count):
            turned[:, c * rows : (c + 1) * rows] = lefts[c][...].T

    total = 0.0
    for s, right in enumerate(rights):
        at = slice(s * each * rows, (s + 1) * each * rows)
        total = total + product(turned[:, at], right[...])
    out[...] = total.astype(low_type)


def weight_gradient(lefts, rights, start, size):
    each, rows = len(lefts[0]), lefts[0][0].shape[0]
    columns, count = rights[0].shape[1], len(lefts) * each
    tile = min(512, size)
    across = next(a for a in (1024, 768, 512, 384, 128) if columns % a == 0)
    first = start // tile
    return pl.pallas_call(
        functools.partial(weight_kernel, count, each),
        grid=(size // tile, columns // across),
        out_shape=jax.ShapeDtypeStruct((size, columns), low_type),
        in_specs=[pl.BlockSpec((rows, tile), lambda m, n: (0, first + m))] * count
        + [pl.BlockSpec((each * rows, across), lambda m, n: (0, n))] * len(rights),
        out_specs=pl.BlockSpec((tile, across), lambda m, n: (m, n)),
        scratch_shapes=[pltpu.VMEM((tile, count * rows), low_type)],
        compiler_params=params(2, 52),
        cost_estimate=brief,
        name="weight_gradient",
    )(*[left for group in lefts for left in group], *rights)


def update_kernel(steps, columns_ref, *refs):
    grads, (w, m, v, g_out, m_out, v_out, w_out) = refs[: len(steps)], refs[len(steps) :]
    step = pl.program_id(0)
    first = 0
    for count, grad_ref in zip(steps, grads):

        @pl.when((step >= first) & (step < first + count))
        def _(grad_ref=grad_ref):
            gradient = grad_ref[...].astype(jnp.float32)
            moment, square, weight = adamw(
                w[...], m[...], v[...], gradient, learn_rate, weight_decay
            )
            g_out[...] = gradient
            m_out[...] = moment
            v_out[...] = square
            w_out[...] = weight

        first += count


def update(grads, columns, across, weight, moment, square):
    rows, width = weight.shape
    steps = [g.shape[0] // rows * (g.shape[1] // across) for g in grads]
    specs, first = [], 0
    for g, count in zip(grads, steps):
        per = g.shape[1] // across

        def place(i, c, first=first, count=count, per=per):
            at = jnp.clip(i - first, 0, count - 1)
            return at // per, at % per

        specs.append(pl.BlockSpec((rows, across), place))
        first += count
    here = pl.BlockSpec((rows, across), lambda i, c: (0, c[i]))
    return pl.pallas_call(
        functools.partial(update_kernel, steps),
        out_shape=(jax.ShapeDtypeStruct((rows, width), jnp.float32),) * 4,
        grid_spec=pltpu.PrefetchScalarGridSpec(
            num_scalar_prefetch=1,
            grid=(sum(steps),),
            in_specs=specs + [here] * 3,
            out_specs=(here,) * 4,
        ),
        compiler_params=params(1, 40),
        cost_estimate=brief,
        name="update",
    )(columns, *grads, weight, moment, square)


def swap(value, axis, bits):
    size = lax.axis_size(axis)
    return lax.ppermute(value, axis, [(i, i ^ bits) for i in range(size)])


def pick(pieces, index):
    return lax.dynamic_index_in_dim(pieces, index, axis=0, keepdims=False)


def trade(pieces, axis):
    size, me = lax.axis_size(axis), lax.axis_index(axis)
    mine = pick(pieces, me)
    out = jnp.zeros((size,) + mine.shape, mine.dtype)
    out = lax.dynamic_update_index_in_dim(out, mine, me, 0)
    for bits in range(1, size):
        got = swap(pick(pieces, me ^ bits), axis, bits)
        out = lax.dynamic_update_index_in_dim(out, got, me ^ bits, 0)
    return out


def trade_near(pieces, axis):
    return [pieces[0]] + [swap(pieces[k], axis, k) for k in range(1, lax.axis_size(axis))]


def after(value, *others):
    return lax.optimization_barrier((value,) + others)[0]


def total_of(value, axes):
    for axis in axes:
        bits = 1
        while bits < lax.axis_size(axis):
            value = value + swap(value, axis, bits)
            bits *= 2
    return value


def gather_pairs(value, axis):
    size, me = lax.axis_size(axis), lax.axis_index(axis)
    bits, value = size // 2, value[None]
    while bits:
        other = swap(value, axis, bits)
        low = (me & bits) == 0
        value = jnp.stack([jnp.where(low, value, other), jnp.where(low, other, value)], axis=1)
        value = value.reshape((-1,) + value.shape[2:])
        bits //= 2
    return value


def sum_pairs(pieces, axis):
    size, me = lax.axis_size(axis), lax.axis_index(axis)
    bits = 1
    while bits < size:
        pieces = pieces.reshape((-1, 2) + pieces.shape[1:])
        mine = (me & bits) // bits
        keep = lax.dynamic_index_in_dim(pieces, mine, axis=1, keepdims=False)
        send = lax.dynamic_index_in_dim(pieces, 1 - mine, axis=1, keepdims=False)
        got = swap(send, axis, bits)
        pieces = (keep.astype(jnp.float32) + got.astype(jnp.float32)).astype(pieces.dtype)
        bits *= 2
    return pieces[0]


def near_order(size):
    return list(range(1, size, 2)) + list(range(0, size, 2))


def gather_group(value, axis):
    size = lax.axis_size(axis)
    got, bits = {0: value}, size // 2
    while bits:
        for known in sorted(got):
            got[known ^ bits] = swap(got[known], axis, bits)
        bits //= 2
    return [got[k] for k in near_order(size)]


def sum_group(got, kept, axis):
    size = lax.axis_size(axis)
    parts, bits, low = got.shape[0], 2, got.dtype
    shape = (parts, size // 2, -1) + got.shape[2:]
    pieces, got = kept.reshape(shape), got.reshape(shape)
    while bits < size:
        pieces = pieces.reshape((parts, -1, 2) + pieces.shape[2:])
        got = got.reshape(pieces.shape)
        send = pieces[:, :, 1].astype(jnp.float32) + got[:, :, 1].astype(jnp.float32)
        pieces = pieces[:, :, 0].astype(jnp.float32) + got[:, :, 0].astype(jnp.float32)
        got = swap(send.astype(low), axis, bits)
        bits *= 2
    return pieces[:, 0].astype(jnp.float32) + got[:, 0].astype(jnp.float32)


def own_first(parts, axis):
    size, me = lax.axis_size(axis), lax.axis_index(axis)
    bits = 1
    while bits < size:
        parts = [jnp.where((me & bits) == 0, parts[i], parts[i ^ bits]) for i in range(size)]
        bits *= 2
    return jnp.concatenate(parts, axis=1)


def adamw(weight, moment, square, gradient, rate, decay):
    moment_new = beta_first * moment + (1.0 - beta_first) * gradient
    square_new = beta_second * square + (1.0 - beta_second) * gradient * gradient
    fix_first = 1.0 - beta_first**STEP
    fix_second = 1.0 - beta_second**STEP
    update = moment_new / fix_first / (jnp.sqrt(square_new / fix_second) + epsilon_adam)
    return (moment_new, square_new, weight - rate * (update + decay * weight))


def body(
    tokens,
    cotangent,
    pairing,
    attention_weights,
    attention_moment,
    attention_square,
    feed_weights,
    feed_moment,
    feed_square,
    gains,
    gain_moment,
    gain_square,
):
    inputs = tokens[0, 0]
    rows, width = inputs.shape
    dps, ctxs, groups = lax.axis_size("dp"), lax.axis_size("ctx"), lax.axis_size("fsdp")
    ctx = lax.axis_index("ctx")
    block = rows // 2
    length = block * ctxs
    owned = attention_weights.shape[0]
    hidden = feed_weights.shape[1] // 3
    part = hidden // groups
    head_width = width // ctxs
    upstream = cotangent[0, 0].astype(jnp.float32)

    rows_of = (slice(0, block), slice(block, rows))
    orders = (pairing[0, 0], ctxs - 1 - pairing[0, 0])
    turns = [turn_tables(start + jnp.arange(length, dtype=jnp.int32)) for start in (0, length)]

    def feed_columns(own, after):
        own, after = lax.optimization_barrier((own, after))
        own = lax.all_gather(own, "ctx", axis=0, tiled=True)
        return [own] + [swap(own, "dp", bits) for bits in range(1, dps)]

    inputs_all = lax.all_gather(inputs, "ctx", axis=0, tiled=True)
    qkv_low = attention_weights[:, : 3 * width].astype(low_type)
    qkv_low = qkv_low.reshape(owned, 3, ctxs, head_width).transpose(2, 0, 1, 3)
    qkv_low = qkv_low.reshape(ctxs, owned, 3 * head_width)
    feed_low = after(feed_weights, qkv_low).astype(low_type)
    qkv_mine = qkv_low = trade(qkv_low, "ctx")
    feed_low = feed_low.reshape(owned, 3, groups, part).transpose(2, 1, 0, 3)
    feed_low = trade(feed_low, "fsdp").transpose(1, 0, 2, 3).reshape(3, groups * owned, part)
    qkv_low = gather_pairs(gather_pairs(qkv_low, "dp"), "fsdp")
    qkv_low = qkv_low.transpose(1, 2, 0, 3, 4).reshape(width, 3 * head_width)
    out_low = after(attention_weights[:, 3 * width :].astype(low_type), qkv_mine)
    out_low = gather_pairs(gather_pairs(out_low, "ctx"), "dp")
    inputs_all, qkv_low, feed_low, out_low, turns = lax.optimization_barrier(
        (inputs_all, qkv_low, feed_low, out_low, turns)
    )

    gates = feed_columns(feed_low[0], inputs_all)

    others = jnp.arange(ctxs, dtype=jnp.int32) ^ ctx
    spots = [jnp.sum(jnp.where(others[:, None] == jnp.arange(ctxs), o, 0), axis=1) for o in orders]
    qk_gains = jnp.stack(
        [lax.dynamic_slice_in_dim(gains[i], ctx * head_width, head_width) for i in range(2)]
    )
    queries, keys, values = [], [], []
    attended, logs, attended_near = [], [], []
    projs, proj_scales, states, chunks = [], [], [], []
    projected = product(inputs_all, qkv_low)
    pre = [projected[:, i * head_width : (i + 1) * head_width] for i in range(2)]
    squares = after(jnp.stack([jnp.sum(p * p, axis=-1) for p in pre]), gates[0])
    squares = total_of(squares, ("ctx",))
    scales = lax.rsqrt(squares / width + epsilon_norm).T
    for s in range(2):
        q, k, v = prepare(projected, scales, qk_gains, *turns[s], orders[s], s)
        queries.append(q)
        keys.append(k)
        values.append(v)

    def attend(s, last):
        out, log = attend_forward(after(queries[s], last), keys[: s + 1], values[: s + 1], spots[s])
        attended.append(out)
        logs.append(log)
        attended_near.append(jnp.stack(trade_near(out.reshape(ctxs, block, head_width), "ctx")))

    def leave(s, last):
        proj = out_project(after(attended_near[s], last), out_low, others)
        projs.append(proj)
        proj_scales.append(
            lax.rsqrt(jnp.mean(proj * proj, axis=-1, keepdims=True) + epsilon_norm)
        )
        states.append(
            inputs[rows_of[s]].astype(jnp.float32) + proj * proj_scales[s] * gains[2]
        )
        state_low = states[s].astype(low_type)
        state_low = own_first(jnp.split(state_low, dps, axis=1), "dp")
        chunks.append(gather_group(state_low, "fsdp"))

    out_low = gather_pairs(after(out_low, scales), "fsdp")
    out_low = out_low.transpose(1, 2, 0, 3, 4).reshape(width, width)
    attend(0, gates[0])
    ups = feed_columns(feed_low[1], gates[0])
    last = after(attended[0], ups[0])
    downs = feed_columns(feed_low[2], last)
    attend(1, last)
    leave(0, attended[1])
    attended_near[1] = after(attended_near[1], gates[-1])
    leave(1, states[0])

    gate, up, inner = [None] * 2, [None] * 2, [None] * 2
    chunks[0][-1] = after(chunks[0][-1], downs[0])
    gate[0], up[0], inner[0] = gate_up(chunks[0], gates, ups)
    chunks[1][-1] = after(chunks[1][-1], gate[0])
    gate[1], up[1], inner[1] = gate_up(chunks[1], gates, ups)
    outs, grad_downs, gain_downs = [None] * 2, [None] * 2, [None] * 2
    last, halves = inner[0], {}
    for s in (1, 0):
        last = spread([after(inner[s], last)], [downs], 0)
        halves[s, 0] = swap(last, "fsdp", 1)
        halves[s, 1] = spread([after(inner[s], last)], [downs], 1)
        last = after(halves[s, 1], halves[s, 0])
    for s in (1, 0):
        down = own_first(list(sum_group(halves[s, 0], halves[s, 1], "fsdp")), "dp")
        down_scale = lax.rsqrt(jnp.mean(down * down, axis=-1, keepdims=True) + epsilon_norm)
        outs[s] = (states[s] + down * down_scale * gains[3]).astype(low_type)
        grad_down, gain_downs[s] = norm_backward(
            down, down_scale, gains[3], upstream[rows_of[s]]
        )
        grad_down = own_first(jnp.split(grad_down.astype(low_type), dps, axis=1), "dp")
        grad_downs[s] = gather_group(grad_down, "fsdp")
    output_states = jnp.concatenate(outs, axis=0)

    grad_gates, grad_ups, grad_states = [None] * 2, [None] * 2, [None] * 2
    grad_projs, grad_heads, gain_branches = [None] * 2, [None] * 2, [None] * 2
    size = width // dps

    def inward(s, last):
        grad_gates[s], grad_ups[s] = inner_backward(
            grad_downs[s], after(gate[s], last), up[s], downs
        )
        last = after(grad_ups[s], *grad_downs[0])
        last = spread([after(grad_gates[s], last), grad_ups[s]], [gates, ups], 0)
        got = swap(last, "fsdp", 1)
        last = spread([after(grad_gates[s], last), grad_ups[s]], [gates, ups], 1)
        return [got, last], after(last, got)

    def gradient_parts(lefts, rights, which, last):
        lefts = [[after(left[0], last)] + left[1:] for left in lefts]
        found = [weight_gradient(lefts, rights, bits * size, size) for bits in which]
        return found, found[-1]

    def outward(s, sums):
        back = sum_group(*sums, "fsdp")
        grad_states[s] = upstream[rows_of[s]] + own_first(list(back), "dp")
        grad_proj, gain_branches[s] = norm_backward(
            projs[s], proj_scales[s], gains[2], grad_states[s]
        )
        grad_projs[s] = grad_proj.astype(low_type)
        grad_attended = out_back(grad_projs[s], out_low, others)
        grad_heads[s] = jnp.concatenate(trade_near(grad_attended, "ctx"), axis=0)
        return grad_attended

    away, near = range(1, dps), range(1)
    sums, last = inward(1, downs[-1])
    down_away, last = gradient_parts(grad_downs, inner, away, last)
    down_away = [swap(piece, "dp", bits) for bits, piece in zip(away, down_away)]
    lower_sums, last = inward(0, last)
    gate_away, last = gradient_parts(chunks, grad_gates, away, last)
    gate_away = [swap(piece, "dp", bits) for bits, piece in zip(away, gate_away)]
    down_near, last = gradient_parts(grad_downs, inner, near, last)

    def kept_feed(own, others):
        kept = own[0].astype(jnp.float32)
        for other in others:
            kept = kept + other.astype(jnp.float32)
        return kept.astype(low_type)

    def reduce_feed(kept):
        return lax.psum_scatter(kept, "ctx", scatter_dimension=0, tiled=True)

    down_kept = kept_feed(down_near, down_away)
    down_gradient = reduce_feed(down_kept)
    sums[1] = after(sums[1], last, down_kept)
    last = outward(1, sums)
    up_away, last = gradient_parts(chunks, grad_ups, away, last)
    up_away = [swap(piece, "dp", bits) for bits, piece in zip(away, up_away)]
    lower_sums[1] = after(lower_sums[1], last)
    last = outward(0, lower_sums)
    gate_near, last = gradient_parts(chunks, grad_gates, near, last)
    gate_kept = kept_feed(gate_near, gate_away)
    gate_gradient = reduce_feed(gate_kept)
    last = after(last, gate_kept, grad_heads[1])
    up_near, last = gradient_parts(chunks, grad_ups, near, last)
    attended_near[0] = after(attended_near[0], last)
    out_gradient = out_weight(attended_near, grad_projs, others)
    queries[1] = after(queries[1], out_gradient)
    up_kept = kept_feed(up_near, up_away)
    up_gradient = reduce_feed(up_kept)

    out_gradient = out_gradient.reshape(dps, ctxs, groups, owned, width).transpose(2, 0, 1, 3, 4)
    out_gradient = sum_pairs(out_gradient, "fsdp")

    def stream_rows(values, s):
        return values.reshape((ctxs, 2, block) + values.shape[1:])[:, s].reshape(
            (length,) + values.shape[1:]
        )

    added, grad_inputs, grad_projected = (), [None] * 2, [None] * 2
    gain_qk = 0.0
    for s in (1, 0):
        if s == 0:
            out_gradient = sum_pairs(out_gradient, "dp")
            added, grad_part, out_gradient = lax.optimization_barrier(
                (added, grad_part, out_gradient)
            )
            grad_inputs[1] = lax.psum_scatter(grad_part, "ctx", scatter_dimension=0, tiled=True)
        grads = attend_backward(
            queries[s],
            grad_heads[s],
            attended[s],
            logs[s],
            keys[: s + 1],
            values[: s + 1],
            added,
            spots[s],
        )
        if s == 1:
            grads, out_gradient, up_kept, grad_heads[0] = lax.optimization_barrier(
                (grads, out_gradient, up_kept, grad_heads[0])
            )
        added = grads[1:]
        weighted, value_low, dots, gain_sums = restore(
            grads, projected, scales, qk_gains, *turns[s], orders[s], s
        )
        gain_qk = gain_qk + gain_sums
        means = total_of(dots.T, ("ctx",)).T / width
        grad_pre = []
        for i in range(2):
            at = slice(i * head_width, (i + 1) * head_width)
            scale = stream_rows(scales, s)[:, i : i + 1]
            unit = stream_rows(projected, s)[:, at] * scale
            grad_pre.append(
                (scale * (weighted[:, at] - unit * means[:, i : i + 1])).astype(low_type)
            )
        grad_projected[s] = jnp.concatenate(grad_pre + [value_low], axis=1)
        grad_part = against(grad_projected[s], qkv_low).astype(low_type)
    grad_inputs[0] = lax.psum_scatter(grad_part, "ctx", scatter_dimension=0, tiled=True)
    out_gradient = sum_pairs(out_gradient, "ctx")
    input_gradient = jnp.concatenate(
        [grad_states[s] + grad_inputs[s].astype(jnp.float32) for s in range(2)], axis=0
    ).astype(low_type)

    qkv_gradient = weight_gradient(
        [[stream_rows(inputs_all, 0)], [stream_rows(after(inputs_all, grad_part), 1)]],
        grad_projected,
        0,
        width,
    )
    qkv_gradient = qkv_gradient.reshape(dps, ctxs, groups, owned, 3 * head_width)
    qkv_gradient = sum_pairs(sum_pairs(qkv_gradient.transpose(2, 0, 1, 3, 4), "fsdp"), "dp")
    qkv_gradient = jnp.concatenate(
        trade_near([pick(qkv_gradient, ctx ^ k) for k in range(ctxs)], "ctx"), axis=0
    )

    fsdp = lax.axis_index("fsdp")
    feed_pieces = []
    for piece in (gate_gradient, up_gradient, down_gradient):
        piece = piece.reshape(groups, owned, part)
        feed_pieces += trade_near([pick(piece, fsdp ^ k) for k in range(groups)], "fsdp")
    near_columns = jnp.arange(groups, dtype=jnp.int32) ^ fsdp
    feed_columns_of = jnp.concatenate([kind * groups + near_columns for kind in range(3)])
    feed_gradient, feed_moment_new, feed_square_new, feed_weights_new = update(
        [jnp.concatenate(feed_pieces, axis=0)],
        feed_columns_of,
        part,
        feed_weights,
        feed_moment,
        feed_square,
    )
    attention_columns = jnp.concatenate(
        [
            (jnp.arange(3, dtype=jnp.int32)[None, :] * ctxs + others[:, None]).reshape(-1),
            3 * ctxs + jnp.arange(ctxs, dtype=jnp.int32),
        ]
    )
    attention_gradient, attention_moment_new, attention_square_new, attention_weights_new = update(
        [qkv_gradient, out_gradient],
        attention_columns,
        head_width,
        attention_weights,
        attention_moment,
        attention_square,
    )

    wide = lax.dynamic_update_slice(
        jnp.zeros((2, width), jnp.float32), gain_qk, (0, ctx * head_width)
    )
    gain_gradient = total_of(
        jnp.concatenate([wide, jnp.stack([sum(gain_branches), sum(gain_downs)])], axis=0), EVERY
    )
    gain_moment_new, gain_square_new, gains_new = adamw(
        gains, gain_moment, gain_square, gain_gradient, gain_rate, 0.0
    )
    return (
        output_states[None, None],
        input_gradient[None, None],
        attention_gradient,
        attention_moment_new,
        attention_square_new,
        attention_weights_new,
        feed_gradient,
        feed_moment_new,
        feed_square_new,
        feed_weights_new,
        gain_gradient,
        gain_moment_new,
        gain_square_new,
        gains_new,
    )


def solution(mesh):
    token = P("dp", "fsdp", "ctx", None)
    row = P(EVERY, None)
    return jax.shard_map(
        body,
        mesh=mesh,
        in_specs=(token, token, P("dp", "fsdp", None)) + (row,) * 6 + (P(),) * 3,
        out_specs=(token, token) + (row,) * 8 + (P(),) * 4,
        check_vma=False,
    )
```

```python
import functools
import math

import jax
import jax.numpy as jnp
from jax import lax
from jax.experimental import pallas as pl
from jax.experimental.pallas import tpu as pltpu
from jax.sharding import PartitionSpec as P

HEADS = 16
HEAD = 128
STEP = 10

epsilon_norm = 1e-06
rope_base = 500000.0
masked_value = -1e30
beta_first = 0.9
beta_second = 0.95
learn_rate = 0.05
gain_rate = 1.0
weight_decay = 0.1
epsilon_adam = 1e-08

score_scale = HEAD ** (-0.5)
exponent_scale = score_scale * math.log2(math.e)

EVERY = ("dp", "ctx", "fsdp")


def turn_tables(places):
    half = HEAD // 2
    frequency = rope_base ** (-(jnp.arange(half, dtype=jnp.float32) * (2.0 / HEAD)))
    angle = places.astype(jnp.float32)[:, None] * frequency[None, :]
    cosine = jnp.cos(angle)
    sine = jnp.sin(angle)
    return (
        jnp.concatenate([cosine, cosine], axis=-1),
        jnp.concatenate([-sine, sine], axis=-1),
    )


def norm_backward(values, scale, gain, upstream):
    weighted = upstream * gain
    inward = scale * (
        weighted - values * (scale * scale) * jnp.mean(weighted * values, axis=-1, keepdims=True)
    )
    return inward, jnp.sum(upstream * values * scale, axis=0)


def product(left, right):
    return jnp.dot(left, right, preferred_element_type=jnp.float32)


def transposed(left, right):
    return lax.dot_general(
        left, right, (((0,), (0,)), ((), ())), preferred_element_type=jnp.float32
    )


def against(left, right):
    return lax.dot_general(
        left, right, (((1,), (1,)), ((), ())), preferred_element_type=jnp.float32
    )


low_type = jnp.bfloat16


def tile_of(length):
    for tile in (512, 384, 256, 128):
        if length % tile == 0:
            return tile
    return length


brief = pl.CostEstimate(flops=1024, bytes_accessed=1024, transcendentals=0)


class Tied:
    def __init__(self, value, others):
        self.value, self.others = value, []
        for other in others:
            self.others += [other.value] + other.others if isinstance(other, Tied) else [other]


def after(value, *others):
    if isinstance(value, Tied):
        return Tied(value.value, [value] + list(others))
    return Tied(value, others)


def plain(value):
    return value.value if isinstance(value, Tied) else value


def untie(*values):
    others = [o for v in values if isinstance(v, Tied) for o in v.others]
    return [plain(v) for v in values], others


def launch(kernel, scalars, others, grid, in_specs, out_specs, out_shape, scratch_shapes=(), **options):
    skip = len(others)

    def run(*refs):
        kernel(*refs[:scalars], *refs[scalars + skip :])

    call = pl.pallas_call(
        run,
        out_shape=out_shape,
        grid_spec=pltpu.PrefetchScalarGridSpec(
            num_scalar_prefetch=scalars,
            grid=grid,
            in_specs=[pl.BlockSpec(memory_space=pl.ANY)] * skip + list(in_specs),
            out_specs=out_specs,
            scratch_shapes=list(scratch_shapes),
        ),
        **options,
    )
    return lambda *operands: call(*operands[:scalars], *others, *operands[scalars:])


def params(steps, mib):
    return pltpu.CompilerParams(
        dimension_semantics=("arbitrary",) * steps, vmem_limit_bytes=mib * 2**20
    )


def prepare_kernel(order_ref, q_ref, k_ref, v_ref, scale_ref, gain_ref, cos_ref, sin_ref, qo, ko, vo):
    cosine, sine = cos_ref[...], sin_ref[...]
    for which, (source, target) in enumerate(((q_ref, qo), (k_ref, ko))):
        scale = scale_ref[:, which : which + 1]
        for start in range(0, source.shape[1], HEAD):
            at = slice(start, start + HEAD)
            part = source[:, at] * scale * gain_ref[which : which + 1, at]
            turned = part * cosine + pltpu.roll(part, HEAD // 2, 1) * sine
            target[:, at] = turned.astype(low_type)
    vo[...] = v_ref[...].astype(low_type)


def prepare(projected, scales, gains, cosine, sine, order, stream):
    length, width = projected.shape[0] // 2, projected.shape[1] // 3
    count = order.shape[0]
    block = length // count
    out = pl.BlockSpec((block, width), lambda b, o: (o[b], 0))
    turn = pl.BlockSpec((block, HEAD), lambda b, o: (o[b], 0))
    return pl.pallas_call(
        prepare_kernel,
        out_shape=(jax.ShapeDtypeStruct((length, width), low_type),) * 3,
        grid_spec=pltpu.PrefetchScalarGridSpec(
            num_scalar_prefetch=1,
            grid=(count,),
            in_specs=[
                pl.BlockSpec((block, width), lambda b, o: (2 * b + stream, 0)),
                pl.BlockSpec((block, width), lambda b, o: (2 * b + stream, 1)),
                pl.BlockSpec((block, width), lambda b, o: (2 * b + stream, 2)),
                pl.BlockSpec((block, 2), lambda b, o: (2 * b + stream, 0)),
                pl.BlockSpec((2, width), lambda b, o: (0, 0)),
                turn,
                turn,
            ],
            out_specs=(out, out, out),
        ),
        compiler_params=params(1, 32),
        cost_estimate=brief,
        name="prepare",
    )(order, projected, projected, projected, scales, gains, cosine, sine)


def restore_kernel(
    order_ref,
    dq_ref,
    dk_ref,
    dv_ref,
    q_ref,
    k_ref,
    scale_ref,
    gain_ref,
    cos_ref,
    sin_ref,
    out_ref,
    value_ref,
    dot_ref,
    sum_ref,
):
    cosine, sine = cos_ref[...] * score_scale, sin_ref[...] * score_scale
    width = q_ref.shape[1]

    @pl.when(pl.program_id(0) == 0)
    def _():
        sum_ref[...] = jnp.zeros_like(sum_ref)

    for which, (source, pre) in enumerate(((dq_ref, q_ref), (dk_ref, k_ref))):
        scale = scale_ref[:, which : which + 1]
        dots = 0.0
        for start in range(0, width, HEAD):
            at = slice(start, start + HEAD)
            part = source[:, at]
            turned = part * cosine - pltpu.roll(part, HEAD // 2, 1) * sine
            weighted = turned * gain_ref[which : which + 1, at]
            unit = pre[:, at] * scale
            out_ref[:, which * width + start : which * width + start + HEAD] = weighted
            dots = dots + jnp.sum(weighted * unit, axis=1, keepdims=True)
            sum_ref[which : which + 1, at] += jnp.sum(turned * unit, axis=0, keepdims=True)
        dot_ref[:, which : which + 1] = dots
    value_ref[...] = dv_ref[...].astype(low_type)


def restore(grads, projected, scales, gains, cosine, sine, order, stream):
    length, width = grads[0].shape
    count = order.shape[0]
    block = length // count
    first = stream * count
    later = pl.BlockSpec((block, width), lambda b, o: (first + o[b], 0))
    turn = pl.BlockSpec((block, HEAD), lambda b, o: (o[b], 0))
    both = pl.BlockSpec((block, 2), lambda b, o: (b, 0))
    scale = pl.BlockSpec((block, 2), lambda b, o: (2 * b + stream, 0))
    small = pl.BlockSpec((2, width), lambda b, o: (0, 0))
    return pl.pallas_call(
        restore_kernel,
        out_shape=(
            jax.ShapeDtypeStruct((length, 2 * width), jnp.float32),
            jax.ShapeDtypeStruct((length, width), low_type),
            jax.ShapeDtypeStruct((length, 2), jnp.float32),
            jax.ShapeDtypeStruct((2, width), jnp.float32),
        ),
        grid_spec=pltpu.PrefetchScalarGridSpec(
            num_scalar_prefetch=1,
            grid=(count,),
            in_specs=[
                pl.BlockSpec((block, width), lambda b, o: (o[b], 0)),
                later,
                later,
                pl.BlockSpec((block, width), lambda b, o: (2 * b + stream, 0)),
                pl.BlockSpec((block, width), lambda b, o: (2 * b + stream, 1)),
                scale,
                small,
                turn,
                turn,
            ],
            out_specs=(
                pl.BlockSpec((block, 2 * width), lambda b, o: (b, 0)),
                pl.BlockSpec((block, width), lambda b, o: (b, 0)),
                both,
                small,
            ),
        ),
        compiler_params=params(1, 40),
        cost_estimate=brief,
        name="restore",
    )(order, *grads, projected, projected, scales, gains, cosine, sine)


def finish_kernel(weighted_ref, q_ref, k_ref, scale_ref, mean_ref, value_ref, out_ref):
    width = q_ref.shape[1]
    for which, pre in enumerate((q_ref, k_ref)):
        at = slice(which * width, (which + 1) * width)
        scale = scale_ref[:, which : which + 1]
        unit = pre[...] * scale
        inward = scale * (weighted_ref[:, at] - unit * mean_ref[:, which : which + 1])
        out_ref[:, at] = inward.astype(low_type)
    out_ref[:, 2 * width :] = value_ref[...]


def finish(weighted, projected, scales, means, values, count, stream):
    length, width = values.shape
    block = length // count
    scale = pl.BlockSpec((block, 2), lambda b: (2 * b + stream, 0))
    return launch(
        finish_kernel,
        0,
        [],
        grid=(count,),
        out_shape=jax.ShapeDtypeStruct((length, 3 * width), low_type),
        in_specs=[
            pl.BlockSpec((block, 2 * width), lambda b: (b, 0)),
            pl.BlockSpec((block, width), lambda b: (2 * b + stream, 0)),
            pl.BlockSpec((block, width), lambda b: (2 * b + stream, 1)),
            scale,
            pl.BlockSpec((block, 2), lambda b: (b, 0)),
            pl.BlockSpec((block, width), lambda b: (b, 0)),
        ],
        out_specs=pl.BlockSpec((block, 3 * width), lambda b: (b, 0)),
        compiler_params=params(1, 40),
        cost_estimate=brief,
        name="finish",
    )(weighted, projected, projected, scales, means, values)


def causal(tile):
    key = lax.broadcasted_iota(jnp.int32, (tile, tile), 0)
    query = lax.broadcasted_iota(jnp.int32, (tile, tile), 1)
    return key <= query


def forward_kernel(tile, parts, spots_ref, q_ref, *refs):
    k_refs, v_refs = refs[:parts], refs[parts : 2 * parts]
    o_ref, log_ref, ks, vt, held_rows = refs[2 * parts :]
    rows = k_refs[0].shape[0]
    step = pl.program_id(1)

    @pl.when(step == 0)
    def _():
        for part in range(parts):
            ks[part * rows : (part + 1) * rows, :] = k_refs[part][...]
            for start in range(0, rows, tile):
                at = slice(part * rows + start, part * rows + start + tile)
                value = v_refs[part][start : start + tile, :]
                vt[:, at] = value.astype(jnp.float32).T.astype(low_type)

    query = q_ref[...]

    def visit(j, carry, masked):
        top, mass, held = carry
        at = pl.ds(pl.multiple_of(j * tile, tile), tile)
        scores = against(ks[at, :], query)
        if masked:
            scores = jnp.where(causal(tile), scores, masked_value)
        new_top = jnp.maximum(top, jnp.max(scores, axis=0, keepdims=True))
        weights = jnp.exp2((scores - new_top) * exponent_scale)
        fade = jnp.exp2((top - new_top) * exponent_scale)
        mass = mass * fade + jnp.sum(weights, axis=0, keepdims=True)
        held = held * fade + product(vt[:, at], weights.astype(low_type))
        return new_top, mass, held

    start = (
        jnp.full((1, tile), masked_value, jnp.float32),
        jnp.zeros((1, tile), jnp.float32),
        jnp.zeros((HEAD, tile), jnp.float32),
    )
    last = step + (parts - 1) * (rows // tile)
    carry = visit(last, start, True)
    top, mass, held = lax.fori_loop(0, last, lambda j, c: visit(j, c, False), carry)
    here = pl.ds(pl.multiple_of(step * tile, tile), tile)
    held_rows[here, :] = (held / mass).T.astype(low_type)
    log_ref[0] = top * exponent_scale + jnp.log2(mass)

    @pl.when(step == rows // tile - 1)
    def _():
        count = spots_ref.shape[0]
        block = rows // count
        for k in range(count):
            there = pl.ds(pl.multiple_of(spots_ref[k] * block, block), block)
            o_ref[k * block : (k + 1) * block, :] = held_rows[there, :]


def attend_forward(queries, keys, values, spots):
    (queries,), others = untie(queries)
    length, width = queries.shape
    heads, parts = width // HEAD, len(keys)
    tile = tile_of(length)
    whole = pl.BlockSpec((length, HEAD), lambda h, i, o: (0, h))
    piece = pl.BlockSpec((tile, HEAD), lambda h, i, o: (i, h))
    return launch(
        functools.partial(forward_kernel, tile, parts),
        1,
        others,
        out_shape=(
            jax.ShapeDtypeStruct((length, width), low_type),
            jax.ShapeDtypeStruct((heads, 1, length), jnp.float32),
        ),
        grid=(heads, length // tile),
        in_specs=[piece] + [whole] * (2 * parts),
        out_specs=(whole, pl.BlockSpec((1, 1, tile), lambda h, i, o: (h, 0, i))),
        scratch_shapes=[
            pltpu.VMEM((parts * length, HEAD), low_type),
            pltpu.VMEM((HEAD, parts * length), low_type),
            pltpu.VMEM((length, HEAD), low_type),
        ],
        compiler_params=params(2, 40),
        cost_estimate=brief,
        name="attend_forward",
    )(spots, queries, *keys, *values)


def backward_kernel(tile, parts, extra, spots_ref, q_ref, g_ref, o_ref, log_ref, *refs):
    k_refs, v_refs = refs[:parts], refs[parts : 2 * parts]
    added = refs[2 * parts : 2 * parts + extra]
    dq_ref, dk_ref, dv_ref, ks, vs, kt, gs, os, delta, dqt = refs[2 * parts + extra :]
    rows = q_ref.shape[0]
    steps = rows // tile
    step = pl.program_id(1)

    @pl.when(step == 0)
    def _():
        for part in range(parts):
            ks[part * rows : (part + 1) * rows, :] = k_refs[part][...]
            vs[part * rows : (part + 1) * rows, :] = v_refs[part][...]
            for start in range(0, rows, tile):
                at = slice(part * rows + start, part * rows + start + tile)
                key = k_refs[part][start : start + tile, :]
                kt[:, at] = key.astype(jnp.float32).T.astype(low_type)
        count = spots_ref.shape[0]
        block = rows // count
        for k in range(count):
            there = pl.ds(pl.multiple_of(spots_ref[k] * block, block), block)
            gs[there, :] = g_ref[k * block : (k + 1) * block, :]
            os[there, :] = o_ref[k * block : (k + 1) * block, :]
        for start in range(0, rows, tile):
            at = slice(start, start + tile)
            both = gs[at, :].astype(jnp.float32) * os[at, :].astype(jnp.float32)
            delta[:, at] = jnp.sum(both.T, axis=0, keepdims=True)
        dqt[...] = jnp.zeros_like(dqt)

    here = pl.ds(pl.multiple_of(step * tile, tile), tile)
    key, value, key_turned = ks[here, :], vs[here, :], kt[:, here]

    def visit(i, carry, masked):
        key_sum, value_sum = carry
        at = pl.ds(pl.multiple_of(i * tile, tile), tile)
        query, outward = q_ref[at, :], gs[at, :]
        scores = against(key, query)
        exact = jnp.exp2(scores * exponent_scale - log_ref[0, :, at])
        if masked:
            exact = jnp.where(causal(tile), exact, 0.0)
        slope = (exact * (against(value, outward) - delta[:, at])).astype(low_type)
        value_sum = value_sum + product(exact.astype(low_type), outward)
        key_sum = key_sum + product(slope, query)
        dqt[:, at] += product(key_turned, slope)
        return key_sum, value_sum

    if extra:
        carry = (added[0][...], added[1][...])
    else:
        carry = (jnp.zeros((tile, HEAD), jnp.float32),) * 2
    own = step - (parts - 1) * steps

    def store(carry):
        dk_ref[...], dv_ref[...] = carry

    @pl.when(own < 0)
    def _():
        store(lax.fori_loop(0, steps, lambda i, c: visit(i, c, False), carry))

    @pl.when(own >= 0)
    def _():
        first = visit(own, carry, True)
        store(lax.fori_loop(own + 1, steps, lambda i, c: visit(i, c, False), first))

    @pl.when(own == steps - 1)
    def _():
        for start in range(0, rows, tile):
            at = slice(start, start + tile)
            dq_ref[at, :] = dqt[:, at].T


def attend_backward(queries, outward, attended, logs, keys, values, added, spots):
    (queries,), others = untie(queries)
    length, width = queries.shape
    heads, parts = width // HEAD, len(keys)
    tile = tile_of(length)
    whole = pl.BlockSpec((length, HEAD), lambda h, j, o: (0, h))
    piece = pl.BlockSpec((tile, HEAD), lambda h, j, o: (j, h))
    total = parts * length
    return launch(
        functools.partial(backward_kernel, tile, parts, len(added)),
        1,
        others,
        out_shape=(
            jax.ShapeDtypeStruct((length, width), jnp.float32),
            jax.ShapeDtypeStruct((total, width), jnp.float32),
            jax.ShapeDtypeStruct((total, width), jnp.float32),
        ),
        grid=(heads, total // tile),
        in_specs=[whole] * 3
        + [pl.BlockSpec((1, 1, length), lambda h, j, o: (h, 0, 0))]
        + [whole] * (2 * parts)
        + [piece] * len(added),
        out_specs=(whole, piece, piece),
        scratch_shapes=[
            pltpu.VMEM((total, HEAD), low_type),
            pltpu.VMEM((total, HEAD), low_type),
            pltpu.VMEM((HEAD, total), low_type),
            pltpu.VMEM((length, HEAD), low_type),
            pltpu.VMEM((length, HEAD), low_type),
            pltpu.VMEM((1, length), jnp.float32),
            pltpu.VMEM((HEAD, length), jnp.float32),
        ],
        compiler_params=params(2, 48),
        cost_estimate=brief,
        name="attend_backward",
    )(spots, queries, outward, attended, logs, *keys, *values, *added)


def out_kernel(others_ref, x_ref, w_ref, out_ref):
    @pl.when(pl.program_id(1) == 0)
    def _():
        out_ref[...] = jnp.zeros_like(out_ref)

    out_ref[...] += product(x_ref[0], w_ref[...])


def out_project(pieces, weight, spots):
    (pieces,), others = untie(pieces)
    count, rows, depth = pieces.shape
    width = weight.shape[1]
    across = min(1024, width)
    return launch(
        out_kernel,
        1,
        others,
        out_shape=jax.ShapeDtypeStruct((rows, width), jnp.float32),
        grid=(width // across, count),
        in_specs=[
            pl.BlockSpec((1, rows, depth), lambda n, k, o: (k, 0, 0)),
            pl.BlockSpec((depth, across), lambda n, k, o: (o[k], n)),
        ],
        out_specs=pl.BlockSpec((rows, across), lambda n, k, o: (0, n)),
        compiler_params=params(2, 32),
        cost_estimate=brief,
        name="out_project",
    )(spots, pieces, weight)


def weave_kernel(odd_ref, own_ref, other_ref, out_ref):
    odd = odd_ref[0]
    for high in range(own_ref.shape[0]):
        out_ref[0, 0, 2 * high + odd] = own_ref[high, 0, 0]
        out_ref[0, 0, 2 * high + 1 - odd] = other_ref[high, 0, 0]


def weave(own, other, odd):
    half, dps, ctxs, rows, width = own.shape
    piece = pl.BlockSpec((half, 1, 1, rows, width), lambda i, j, o: (0, i, j, 0, 0))
    return pl.pallas_call(
        weave_kernel,
        out_shape=jax.ShapeDtypeStruct((dps, ctxs, 2 * half, rows, width), own.dtype),
        grid_spec=pltpu.PrefetchScalarGridSpec(
            num_scalar_prefetch=1,
            grid=(dps, ctxs),
            in_specs=[piece, piece],
            out_specs=pl.BlockSpec(
                (1, 1, 2 * half, rows, width), lambda i, j, o: (i, j, 0, 0, 0)
            ),
        ),
        compiler_params=params(2, 32),
        cost_estimate=brief,
        name="weave",
    )(odd, own, other)


def out_back_kernel(others_ref, x_ref, w_ref, out_ref):
    out_ref[0] = against(x_ref[...], w_ref[...]).astype(low_type)


def out_back(grad, weight, spots):
    (grad,), others = untie(grad)
    rows, width = grad.shape
    count = spots.shape[0]
    depth = weight.shape[0] // count
    return launch(
        out_back_kernel,
        1,
        others,
        out_shape=jax.ShapeDtypeStruct((count, rows, depth), low_type),
        grid=(count,),
        in_specs=[
            pl.BlockSpec((rows, width), lambda k, o: (0, 0)),
            pl.BlockSpec((depth, width), lambda k, o: (o[k], 0)),
        ],
        out_specs=pl.BlockSpec((1, rows, depth), lambda k, o: (k, 0, 0)),
        compiler_params=params(1, 32),
        cost_estimate=brief,
        name="out_back",
    )(spots, grad, weight)


def out_weight_kernel(streams, others_ref, *refs):
    lefts, rights, out_ref = refs[:streams], refs[streams:-1], refs[-1]
    total = 0.0
    for left, right in zip(lefts, rights):
        total = total + product(left[0].T, right[...])
    out_ref[...] = total.astype(low_type)


def out_weight(lefts, rights, spots):
    lefts, others = untie(*lefts)
    count, rows, depth = lefts[0].shape
    width = rights[0].shape[1]
    across = min(1024, width)
    return launch(
        functools.partial(out_weight_kernel, len(lefts)),
        1,
        others,
        out_shape=jax.ShapeDtypeStruct((count * depth, width), low_type),
        grid=(width // across, count),
        in_specs=[pl.BlockSpec((1, rows, depth), lambda n, k, o: (k, 0, 0))] * len(lefts)
        + [pl.BlockSpec((rows, across), lambda n, k, o: (0, n))] * len(rights),
        out_specs=pl.BlockSpec((depth, across), lambda n, k, o: (o[k], n)),
        compiler_params=params(2, 32),
        cost_estimate=brief,
        name="out_weight",
    )(spots, *lefts, *rights)


def chosen(refs, index, use):
    for i, ref in enumerate(refs):
        pl.when(index == i)(functools.partial(use, ref))


def gate_up_kernel(count, parts, *refs):
    pieces, refs = refs[:count], refs[count:]
    gates, ups = refs[:parts], refs[parts : 2 * parts]
    gate_ref, up_ref, inner_ref = refs[2 * parts :]
    half = pieces[0].shape[1] // parts

    def use(x_ref):
        gate = up = 0.0
        for p in range(parts):
            piece = x_ref[:, p * half : (p + 1) * half]
            gate = gate + product(piece, gates[p][...])
            up = up + product(piece, ups[p][...])
        gate_ref[...] = gate.astype(low_type)
        up_ref[...] = up.astype(low_type)
        inner_ref[...] = (gate * jax.nn.sigmoid(gate) * up).astype(low_type)

    chosen(pieces, pl.program_id(1), use)


def gate_up(pieces, gates, ups):
    pieces, others = untie(*pieces)
    count, (rows, width) = len(pieces), pieces[0].shape
    parts, columns = len(gates), gates[0].shape[1]
    across = min(512, columns)
    weight = pl.BlockSpec((width // parts, across), lambda n, m: (0, n))
    out = pl.BlockSpec((rows, across), lambda n, m: (m, n))
    return launch(
        functools.partial(gate_up_kernel, count, parts),
        0,
        others,
        grid=(columns // across, count),
        out_shape=(jax.ShapeDtypeStruct((count * rows, columns), low_type),) * 3,
        in_specs=[pl.BlockSpec((rows, width), lambda n, m: (0, 0))] * count
        + [weight] * (2 * parts),
        out_specs=(out,) * 3,
        compiler_params=params(2, 52),
        cost_estimate=brief,
        name="gate_up",
    )(*pieces, *gates, *ups)


def spread_kernel(terms, parts, *refs):
    lefts, weights, out = refs[:terms], refs[terms:-1], refs[-1]
    for p in range(parts):
        total = 0.0
        for t in range(terms):
            total = total + against(lefts[t][...], weights[t * parts + p][...])
        out[p] = total.astype(low_type)


def spread(lefts, weights, half):
    lefts, others = untie(*lefts)
    rows, columns = lefts[0].shape[0] // 2, lefts[0].shape[1]
    terms, parts, features = len(lefts), len(weights[0]), weights[0][0].shape[0]
    across = min(256, features)
    return launch(
        functools.partial(spread_kernel, terms, parts),
        0,
        others,
        grid=(features // across,),
        out_shape=jax.ShapeDtypeStruct((parts, rows, features), low_type),
        in_specs=[pl.BlockSpec((rows, columns), lambda n: (half, 0))] * terms
        + [pl.BlockSpec((across, columns), lambda n: (n, 0))] * (terms * parts),
        out_specs=pl.BlockSpec((parts, rows, across), lambda n: (0, 0, n)),
        compiler_params=params(1, 52),
        cost_estimate=brief,
        name="spread",
    )(*lefts, *[w for group in weights for w in group])


def inner_kernel(count, parts, *refs):
    pieces, (gate_ref, up_ref), refs = refs[:count], refs[count : count + 2], refs[count + 2 :]
    weights, (dgate_ref, dup_ref) = refs[:parts], refs[parts:]
    half = pieces[0].shape[1] // parts

    def use(x_ref):
        grad = 0.0
        for p in range(parts):
            grad = grad + product(x_ref[:, p * half : (p + 1) * half], weights[p][...])
        gate, up = gate_ref[...].astype(jnp.float32), up_ref[...].astype(jnp.float32)
        sigma = jax.nn.sigmoid(gate)
        dgate_ref[...] = (grad * up * sigma * (1.0 + gate * (1.0 - sigma))).astype(low_type)
        dup_ref[...] = (grad * gate * sigma).astype(low_type)

    chosen(pieces, pl.program_id(1), use)


def inner_backward(pieces, gate, up, downs):
    (gate,), others = untie(gate)
    count, (rows, width) = len(pieces), pieces[0].shape
    parts, columns = len(downs), downs[0].shape[1]
    across = min(1024, columns)
    out = pl.BlockSpec((rows, across), lambda n, m: (m, n))
    return launch(
        functools.partial(inner_kernel, count, parts),
        0,
        others,
        grid=(columns // across, count),
        out_shape=(jax.ShapeDtypeStruct((count * rows, columns), low_type),) * 2,
        in_specs=[pl.BlockSpec((rows, width), lambda n, m: (0, 0))] * count
        + [out, out]
        + [pl.BlockSpec((width // parts, across), lambda n, m: (0, n))] * parts,
        out_specs=(out,) * 2,
        compiler_params=params(2, 52),
        cost_estimate=brief,
        name="inner_backward",
    )(*pieces, gate, up, *downs)


def weight_kernel(count, each, *refs):
    lefts, rights, (out, turned) = refs[:count], refs[count : count + count // each], refs[-2:]
    rows = lefts[0].shape[0]

    @pl.when(pl.program_id(1) == 0)
    def _():
        for c in range(count):
            turned[:, c * rows : (c + 1) * rows] = lefts[c][...].T

    total = 0.0
    for s, right in enumerate(rights):
        at = slice(s * each * rows, (s + 1) * each * rows)
        total = total + product(turned[:, at], right[...])
    out[...] = total.astype(low_type)


def weight_gradient(lefts, rights, start, size):
    lefts, others = [list(left) for left in lefts], untie(*[v for left in lefts for v in left])[1]
    lefts = [[plain(v) for v in left] for left in lefts]
    each, rows = len(lefts[0]), lefts[0][0].shape[0]
    columns, count = rights[0].shape[1], len(lefts) * each
    tile = min(512, size)
    across = next(a for a in (1024, 768, 512, 384, 128) if columns % a == 0)
    first = start // tile
    return launch(
        functools.partial(weight_kernel, count, each),
        0,
        others,
        grid=(size // tile, columns // across),
        out_shape=jax.ShapeDtypeStruct((size, columns), low_type),
        in_specs=[pl.BlockSpec((rows, tile), lambda m, n: (0, first + m))] * count
        + [pl.BlockSpec((each * rows, across), lambda m, n: (0, n))] * len(rights),
        out_specs=pl.BlockSpec((tile, across), lambda m, n: (m, n)),
        scratch_shapes=[pltpu.VMEM((tile, count * rows), low_type)],
        compiler_params=params(2, 52),
        cost_estimate=brief,
        name="weight_gradient",
    )(*[left for group in lefts for left in group], *rights)


def update_kernel(steps, columns_ref, *refs):
    grads, (w, m, v, g_out, m_out, v_out, w_out) = refs[: len(steps)], refs[len(steps) :]
    step = pl.program_id(0)
    first = 0
    for count, grad_ref in zip(steps, grads):

        @pl.when((step >= first) & (step < first + count))
        def _(grad_ref=grad_ref):
            gradient = grad_ref[...].astype(jnp.float32)
            moment, square, weight = adamw(
                w[...], m[...], v[...], gradient, learn_rate, weight_decay
            )
            g_out[...] = gradient
            m_out[...] = moment
            v_out[...] = square
            w_out[...] = weight

        first += count


def update(grads, columns, across, weight, moment, square):
    rows, width = weight.shape
    steps = [g.shape[0] // rows * (g.shape[1] // across) for g in grads]
    specs, first = [], 0
    for g, count in zip(grads, steps):
        per = g.shape[1] // across

        def place(i, c, first=first, count=count, per=per):
            at = jnp.clip(i - first, 0, count - 1)
            return at // per, at % per

        specs.append(pl.BlockSpec((rows, across), place))
        first += count
    here = pl.BlockSpec((rows, across), lambda i, c: (0, c[i]))
    return pl.pallas_call(
        functools.partial(update_kernel, steps),
        out_shape=(jax.ShapeDtypeStruct((rows, width), jnp.float32),) * 4,
        grid_spec=pltpu.PrefetchScalarGridSpec(
            num_scalar_prefetch=1,
            grid=(sum(steps),),
            in_specs=specs + [here] * 3,
            out_specs=(here,) * 4,
        ),
        compiler_params=params(1, 40),
        cost_estimate=brief,
        name="update",
    )(columns, *grads, weight, moment, square)


def swap(value, axis, bits):
    size = lax.axis_size(axis)
    return lax.ppermute(value, axis, [(i, i ^ bits) for i in range(size)])


def pick(pieces, index):
    return lax.dynamic_index_in_dim(pieces, index, axis=0, keepdims=False)


def trade(pieces, axis):
    size, me = lax.axis_size(axis), lax.axis_index(axis)
    mine = pick(pieces, me)
    out = jnp.zeros((size,) + mine.shape, mine.dtype)
    out = lax.dynamic_update_index_in_dim(out, mine, me, 0)
    for bits in range(1, size):
        got = swap(pick(pieces, me ^ bits), axis, bits)
        out = lax.dynamic_update_index_in_dim(out, got, me ^ bits, 0)
    return out


def trade_near(pieces, axis):
    return [pieces[0]] + [swap(pieces[k], axis, k) for k in range(1, lax.axis_size(axis))]


def total_of(value, axes):
    for axis in axes:
        bits = 1
        while bits < lax.axis_size(axis):
            value = value + swap(value, axis, bits)
            bits *= 2
    return value


def gather_pairs(value, axis, stop=0):
    size, me = lax.axis_size(axis), lax.axis_index(axis)
    bits, value = size // 2, value[None]
    while bits > stop:
        other = swap(value, axis, bits)
        low = (me & bits) == 0
        value = jnp.stack([jnp.where(low, value, other), jnp.where(low, other, value)], axis=1)
        value = value.reshape((-1,) + value.shape[2:])
        bits //= 2
    return value


def sum_pairs(pieces, axis):
    size, me = lax.axis_size(axis), lax.axis_index(axis)
    bits = 1
    while bits < size:
        pieces = pieces.reshape((-1, 2) + pieces.shape[1:])
        mine = (me & bits) // bits
        keep = lax.dynamic_index_in_dim(pieces, mine, axis=1, keepdims=False)
        send = lax.dynamic_index_in_dim(pieces, 1 - mine, axis=1, keepdims=False)
        got = swap(send, axis, bits)
        pieces = (keep.astype(jnp.float32) + got.astype(jnp.float32)).astype(pieces.dtype)
        bits *= 2
    return pieces[0]


def near_order(size):
    return list(range(1, size, 2)) + list(range(0, size, 2))


def gather_group(value, axis):
    size = lax.axis_size(axis)
    got, bits = {0: value}, size // 2
    while bits:
        for known in sorted(got):
            got[known ^ bits] = swap(got[known], axis, bits)
        bits //= 2
    return [got[k] for k in near_order(size)]


def sum_group(got, kept, axis):
    size = lax.axis_size(axis)
    parts, bits, low = got.shape[0], 2, got.dtype
    shape = (parts, size // 2, -1) + got.shape[2:]
    pieces, got = kept.reshape(shape), got.reshape(shape)
    while bits < size:
        pieces = pieces.reshape((parts, -1, 2) + pieces.shape[2:])
        got = got.reshape(pieces.shape)
        send = pieces[:, :, 1].astype(jnp.float32) + got[:, :, 1].astype(jnp.float32)
        pieces = pieces[:, :, 0].astype(jnp.float32) + got[:, :, 0].astype(jnp.float32)
        got = swap(send.astype(low), axis, bits)
        bits *= 2
    return pieces[:, 0], got[:, 0]


def joined(terms):
    return list(terms[0].astype(jnp.float32) + terms[1].astype(jnp.float32))


def own_first(parts, axis):
    size, me = lax.axis_size(axis), lax.axis_index(axis)
    bits = 1
    while bits < size:
        parts = [jnp.where((me & bits) == 0, parts[i], parts[i ^ bits]) for i in range(size)]
        bits *= 2
    return jnp.concatenate(parts, axis=1)


def adamw(weight, moment, square, gradient, rate, decay):
    moment_new = beta_first * moment + (1.0 - beta_first) * gradient
    square_new = beta_second * square + (1.0 - beta_second) * gradient * gradient
    fix_first = 1.0 - beta_first**STEP
    fix_second = 1.0 - beta_second**STEP
    update = moment_new / fix_first / (jnp.sqrt(square_new / fix_second) + epsilon_adam)
    return (moment_new, square_new, weight - rate * (update + decay * weight))


def body(
    tokens,
    cotangent,
    pairing,
    attention_weights,
    attention_moment,
    attention_square,
    feed_weights,
    feed_moment,
    feed_square,
    gains,
    gain_moment,
    gain_square,
):
    inputs = tokens[0, 0]
    rows, width = inputs.shape
    dps, ctxs, groups = lax.axis_size("dp"), lax.axis_size("ctx"), lax.axis_size("fsdp")
    ctx = lax.axis_index("ctx")
    block = rows // 2
    length = block * ctxs
    owned = attention_weights.shape[0]
    hidden = feed_weights.shape[1] // 3
    part = hidden // groups
    head_width = width // ctxs
    upstream = cotangent[0, 0].astype(jnp.float32)

    rows_of = (slice(0, block), slice(block, rows))
    orders = (pairing[0, 0], ctxs - 1 - pairing[0, 0])
    turns = [turn_tables(start + jnp.arange(length, dtype=jnp.int32)) for start in (0, length)]

    def own_rows(own):
        return lax.all_gather(own, "ctx", axis=0, tiled=True)

    def both_rows(own):
        return [own] + [swap(own, "dp", bits) for bits in range(1, dps)]

    hold = lax.optimization_barrier
    inputs_all = lax.all_gather(inputs, "ctx", axis=0, tiled=True)
    qkv_low = attention_weights[:, : 3 * width].astype(low_type)
    qkv_low = qkv_low.reshape(owned, 3, ctxs, head_width).transpose(2, 0, 1, 3)
    qkv_low = qkv_low.reshape(ctxs, owned, 3 * head_width)
    feed_low = feed_weights.astype(low_type)
    qkv_low = trade(qkv_low, "ctx")
    feed_low = feed_low.reshape(owned, 3, groups, part).transpose(2, 1, 0, 3)
    feed_low = trade(feed_low, "fsdp").transpose(1, 0, 2, 3).reshape(3, groups * owned, part)
    qkv_low = gather_pairs(gather_pairs(qkv_low, "dp"), "fsdp")
    qkv_low = qkv_low.transpose(1, 2, 0, 3, 4).reshape(width, 3 * head_width)
    out_low = attention_weights[:, 3 * width :].astype(low_type)
    out_low = gather_pairs(gather_pairs(out_low, "ctx"), "dp")
    inputs_all, qkv_low, feed_low, out_low, turns = lax.optimization_barrier(
        (inputs_all, qkv_low, feed_low, out_low, turns)
    )

    near = jnp.arange(ctxs, dtype=jnp.int32) ^ ctx
    spots = [jnp.sum(jnp.where(near[:, None] == jnp.arange(ctxs), o, 0), axis=1) for o in orders]
    qk_gains = jnp.stack(
        [lax.dynamic_slice_in_dim(gains[i], ctx * head_width, head_width) for i in range(2)]
    )
    queries, keys, values = [], [], []
    attended, logs, attended_near = [], [], []
    projs, proj_scales, states, chunks = [], [], [], []
    projected = product(inputs_all, qkv_low)
    feed_own = [feed_low[0], feed_low[1], feed_low[2]]
    feed_own[0] = own_rows(feed_own[0])
    projected, feed_own[0], feed_own[1] = hold((projected, feed_own[0], feed_own[1]))
    gates = both_rows(feed_own[0])
    pre = [projected[:, i * head_width : (i + 1) * head_width] for i in range(2)]
    squares = total_of(jnp.stack([jnp.sum(p * p, axis=-1) for p in pre]), ("ctx",))
    scales = lax.rsqrt(squares / width + epsilon_norm).T
    for s in range(2):
        q, k, v = prepare(projected, scales, qk_gains, *turns[s], orders[s], s)
        queries.append(q)
        keys.append(k)
        values.append(v)

    def attend(s, last):
        out, log = attend_forward(after(queries[s], last), keys[: s + 1], values[: s + 1], spots[s])
        attended.append(out)
        logs.append(log)
        return trade_near(out.reshape(ctxs, block, head_width), "ctx")

    def leave(s, pieces, *others):
        attended_near.append(jnp.stack(pieces))
        proj = out_project(after(attended_near[s], *others), out_low, near)
        projs.append(proj)
        proj_scales.append(
            lax.rsqrt(jnp.mean(proj * proj, axis=-1, keepdims=True) + epsilon_norm)
        )
        states.append(
            inputs[rows_of[s]].astype(jnp.float32) + proj * proj_scales[s] * gains[2]
        )
        state_low = states[s].astype(low_type)
        state_low = own_first(jnp.split(state_low, dps, axis=1), "dp")
        chunks.append(gather_group(state_low, "fsdp"))

    out_low, scales = hold((out_low, scales))
    out_low = gather_pairs(out_low, "fsdp", 1)
    feed_own[1] = own_rows(feed_own[1])
    lower = attend(0, gates[0])
    out_low, feed_own[1], feed_own[2], attended[0] = hold(
        (out_low, feed_own[1], feed_own[2], attended[0])
    )
    out_other = swap(out_low, "fsdp", 1)
    ups = both_rows(feed_own[1])
    feed_own[2] = own_rows(feed_own[2])
    upper = attend(1, after(ups[0], gates[-1]))
    out_other, lower, upper, attended[1] = hold((out_other, lower, upper, attended[1]))
    odd = (lax.axis_index("fsdp") & 1)[None]
    out_low = weave(out_low, out_other, odd).reshape(width, width)
    leave(0, lower, gates[-1], ups[-1])
    leave(1, upper, states[0])
    feed_own[2], states[0] = hold((feed_own[2], states[0]))
    downs = both_rows(feed_own[2])

    gate, up, inner = [None] * 2, [None] * 2, [None] * 2
    outs, grad_downs, gain_downs = [None] * 2, [None] * 2, [None] * 2
    last, sums = downs[0], [None] * 2
    for s in range(2):
        chunks[s][-1] = after(chunks[s][-1], last)
        gate[s], up[s], inner[s] = gate_up(chunks[s], gates, ups)
        last = inner[s]
    for s in range(2):
        last = spread([after(inner[s], last)], [downs], 0)
        got = swap(last, "fsdp", 1)
        last = spread([after(inner[s], last)], [downs], 1)
        sums[s] = sum_group(got, last, "fsdp")
        last = after(last, got)
    for s in range(2):
        if s == 1:
            sums[1], grad_downs[0] = hold((sums[1], grad_downs[0]))
        down = own_first(joined(sums[s]), "dp")
        down_scale = lax.rsqrt(jnp.mean(down * down, axis=-1, keepdims=True) + epsilon_norm)
        outs[s] = (states[s] + down * down_scale * gains[3]).astype(low_type)
        grad_down, gain_downs[s] = norm_backward(
            down, down_scale, gains[3], upstream[rows_of[s]]
        )
        grad_down = own_first(jnp.split(grad_down.astype(low_type), dps, axis=1), "dp")
        grad_downs[s] = gather_group(grad_down, "fsdp")
    output_states = jnp.concatenate(outs, axis=0)

    grad_gates, grad_ups, grad_states = [None] * 2, [None] * 2, [None] * 2
    grad_projs, grad_heads, gain_branches = [None] * 2, [None] * 2, [None] * 2
    size = width // dps

    def inward(s, last):
        grad_gates[s], grad_ups[s] = inner_backward(
            grad_downs[s], after(gate[s], last), up[s], downs
        )
        last = grad_ups[s]
        last = spread([after(grad_gates[s], last), grad_ups[s]], [gates, ups], 0)
        got = swap(last, "fsdp", 1)
        last = spread([after(grad_gates[s], last), grad_ups[s]], [gates, ups], 1)
        return sum_group(got, last, "fsdp"), after(last, got)

    def gradient_parts(lefts, rights, which, last):
        lefts = [[after(left[0], last)] + left[1:] for left in lefts]
        found = [weight_gradient(lefts, rights, bits * size, size) for bits in which]
        return found, found[-1]

    def outward(s, sums):
        grad_states[s] = upstream[rows_of[s]] + own_first(joined(sums), "dp")
        grad_proj, gain_branches[s] = norm_backward(
            projs[s], proj_scales[s], gains[2], grad_states[s]
        )
        grad_projs[s] = grad_proj.astype(low_type)
        grad_attended = out_back(grad_projs[s], out_low, near)
        grad_heads[s] = trade_near(grad_attended, "ctx")
        return grad_attended

    away, own = range(1, dps), range(1)
    def kept_feed(own, others):
        kept = own[0].astype(jnp.float32)
        for other in others:
            kept = kept + other.astype(jnp.float32)
        return kept.astype(low_type)

    def reduce_feed(kept):
        return lax.psum_scatter(kept, "ctx", scatter_dimension=0, tiled=True)

    def exchanged(pieces):
        return [swap(piece, "dp", bits) for bits, piece in zip(away, pieces)]

    away, own = range(1, dps), range(1)
    lower_sums, last = inward(0, downs[-1])
    down_away, last = gradient_parts(grad_downs, inner, away, last)
    down_away = exchanged(down_away)
    upper_sums, last = inward(1, last)
    gate_away, last = gradient_parts(chunks, grad_gates, away, last)
    upper_sums, down_away, gate_away = hold((upper_sums, down_away, gate_away))
    gate_away = exchanged(gate_away)
    last = outward(1, upper_sums)
    down_near, last = gradient_parts(grad_downs, inner, own, last)
    down_kept = kept_feed(down_near, down_away)
    lower_sums, down_kept, grad_heads[1] = hold((lower_sums, down_kept, grad_heads[1]))
    down_gradient = reduce_feed(down_kept)
    last = outward(0, lower_sums)
    up_away, last = gradient_parts(chunks, grad_ups, away, last)
    up_away = exchanged(up_away)
    gate_near, last = gradient_parts(chunks, grad_gates, own, last)
    gate_kept = kept_feed(gate_near, gate_away)
    gate_gradient = reduce_feed(gate_kept)
    up_near, last = gradient_parts(
        chunks, grad_ups, own, after(last, gate_kept, *grad_heads[1])
    )
    queries[1] = after(queries[1], last)
    up_kept = kept_feed(up_near, up_away)
    up_gradient = reduce_feed(up_kept)

    fsdp = lax.axis_index("fsdp")

    def feed_trade(piece):
        piece = piece.reshape(groups, owned, part)
        return trade_near([pick(piece, fsdp ^ k) for k in range(groups)], "fsdp")

    def stream_rows(values, s):
        return values.reshape((ctxs, 2, block) + values.shape[1:])[:, s].reshape(
            (length,) + values.shape[1:]
        )

    added, grad_inputs, grad_projected = (), [None] * 2, [None] * 2
    gain_qk = 0.0
    for s in (1, 0):
        if s == 0:
            down_traded = feed_trade(down_gradient)
            added, grad_part, out_gradient, down_traded = lax.optimization_barrier(
                (added, grad_part, out_gradient, down_traded)
            )
            grad_inputs[1] = lax.psum_scatter(grad_part, "ctx", scatter_dimension=0, tiled=True)
        grads = attend_backward(
            queries[s],
            jnp.concatenate(grad_heads[s], axis=0),
            attended[s],
            logs[s],
            keys[: s + 1],
            values[: s + 1],
            added,
            spots[s],
        )
        if s == 1:
            grads, up_kept, grad_heads[0] = hold((grads, up_kept, grad_heads[0]))
            attended_near[0] = after(attended_near[0], grads[0])
            out_gradient = out_weight(attended_near, grad_projs, near)
            out_gradient = out_gradient.reshape(dps, ctxs, groups, owned, width)
            out_gradient = sum_pairs(out_gradient.transpose(2, 0, 1, 3, 4), "fsdp")
        added = grads[1:]
        weighted, value_low, dots, gain_sums = restore(
            grads, projected, scales, qk_gains, *turns[s], orders[s], s
        )
        gain_qk = gain_qk + gain_sums
        means = total_of(dots.T, ("ctx",)).T / width
        grad_projected[s] = finish(
            weighted, projected, scales, means, value_low, ctxs, s
        )
        if s == 0:
            out_gradient = sum_pairs(out_gradient, "dp")
            gate_gradient, up_gradient, out_gradient, grad_projected[0] = hold(
                (gate_gradient, up_gradient, out_gradient, grad_projected[0])
            )
            gate_traded = feed_trade(gate_gradient)
            up_traded = feed_trade(up_gradient)
            qkv_gradient = weight_gradient(
                [[stream_rows(inputs_all, 0)], [stream_rows(inputs_all, 1)]],
                grad_projected,
                0,
                width,
            )
            grad_projected[0], qkv_gradient = hold((grad_projected[0], qkv_gradient))
        grad_part = against(grad_projected[s], qkv_low).astype(low_type)
    grad_inputs[0] = lax.psum_scatter(grad_part, "ctx", scatter_dimension=0, tiled=True)
    out_gradient = sum_pairs(out_gradient, "ctx")
    input_gradient = jnp.concatenate(
        [grad_states[s] + grad_inputs[s].astype(jnp.float32) for s in range(2)], axis=0
    ).astype(low_type)

    qkv_gradient = qkv_gradient.reshape(dps, ctxs, groups, owned, 3 * head_width)
    qkv_gradient = sum_pairs(sum_pairs(qkv_gradient.transpose(2, 0, 1, 3, 4), "fsdp"), "dp")
    qkv_gradient = jnp.concatenate(
        trade_near([pick(qkv_gradient, ctx ^ k) for k in range(ctxs)], "ctx"), axis=0
    )

    feed_pieces = gate_traded + up_traded + list(down_traded)
    near_columns = jnp.arange(groups, dtype=jnp.int32) ^ fsdp
    feed_columns_of = jnp.concatenate([kind * groups + near_columns for kind in range(3)])
    feed_gradient, feed_moment_new, feed_square_new, feed_weights_new = update(
        [jnp.concatenate(feed_pieces, axis=0)],
        feed_columns_of,
        part,
        feed_weights,
        feed_moment,
        feed_square,
    )
    attention_columns = jnp.concatenate(
        [
            (jnp.arange(3, dtype=jnp.int32)[None, :] * ctxs + near[:, None]).reshape(-1),
            3 * ctxs + jnp.arange(ctxs, dtype=jnp.int32),
        ]
    )
    attention_gradient, attention_moment_new, attention_square_new, attention_weights_new = update(
        [qkv_gradient, out_gradient],
        attention_columns,
        head_width,
        attention_weights,
        attention_moment,
        attention_square,
    )

    wide = lax.dynamic_update_slice(
        jnp.zeros((2, width), jnp.float32), gain_qk, (0, ctx * head_width)
    )
    gain_gradient = total_of(
        jnp.concatenate([wide, jnp.stack([sum(gain_branches), sum(gain_downs)])], axis=0), EVERY
    )
    gain_moment_new, gain_square_new, gains_new = adamw(
        gains, gain_moment, gain_square, gain_gradient, gain_rate, 0.0
    )
    return (
        output_states[None, None],
        input_gradient[None, None],
        attention_gradient,
        attention_moment_new,
        attention_square_new,
        attention_weights_new,
        feed_gradient,
        feed_moment_new,
        feed_square_new,
        feed_weights_new,
        gain_gradient,
        gain_moment_new,
        gain_square_new,
        gains_new,
    )


def solution(mesh):
    token = P("dp", "fsdp", "ctx", None)
    row = P(EVERY, None)
    return jax.shard_map(
        body,
        mesh=mesh,
        in_specs=(token, token, P("dp", "fsdp", None)) + (row,) * 6 + (P(),) * 3,
        out_specs=(token, token) + (row,) * 8 + (P(),) * 4,
        check_vma=False,
    )
```

```python
import functools
import math

import jax
import jax.numpy as jnp
from jax import lax
from jax.experimental import pallas as pl
from jax.experimental.pallas import tpu as pltpu
from jax.sharding import PartitionSpec as P

HEADS = 16
HEAD = 128
STEP = 10

epsilon_norm = 1e-06
rope_base = 500000.0
masked_value = -1e30
beta_first = 0.9
beta_second = 0.95
learn_rate = 0.05
gain_rate = 1.0
weight_decay = 0.1
epsilon_adam = 1e-08

score_scale = HEAD ** (-0.5)
exponent_scale = score_scale * math.log2(math.e)

EVERY = ("dp", "ctx", "fsdp")


def turn_tables(places):
    half = HEAD // 2
    frequency = rope_base ** (-(jnp.arange(half, dtype=jnp.float32) * (2.0 / HEAD)))
    angle = places.astype(jnp.float32)[:, None] * frequency[None, :]
    cosine = jnp.cos(angle)
    sine = jnp.sin(angle)
    return (
        jnp.concatenate([cosine, cosine], axis=-1),
        jnp.concatenate([-sine, sine], axis=-1),
    )


def norm_backward(values, scale, gain, upstream):
    weighted = upstream * gain
    inward = scale * (
        weighted - values * (scale * scale) * jnp.mean(weighted * values, axis=-1, keepdims=True)
    )
    return inward, jnp.sum(upstream * values * scale, axis=0)


def product(left, right):
    return jnp.dot(left, right, preferred_element_type=jnp.float32)


def transposed(left, right):
    return lax.dot_general(
        left, right, (((0,), (0,)), ((), ())), preferred_element_type=jnp.float32
    )


def against(left, right):
    return lax.dot_general(
        left, right, (((1,), (1,)), ((), ())), preferred_element_type=jnp.float32
    )


low_type = jnp.bfloat16


def tile_of(length):
    for tile in (512, 384, 256, 128):
        if length % tile == 0:
            return tile
    return length


brief = pl.CostEstimate(flops=1024, bytes_accessed=1024, transcendentals=0)


class Tied:
    def __init__(self, value, others):
        self.value, self.others = value, []
        for other in others:
            self.others += [other.value] + other.others if isinstance(other, Tied) else [other]


def after(value, *others):
    if isinstance(value, Tied):
        return Tied(value.value, [value] + list(others))
    return Tied(value, others)


def plain(value):
    return value.value if isinstance(value, Tied) else value


def untie(*values):
    others = [o for v in values if isinstance(v, Tied) for o in v.others]
    return [plain(v) for v in values], others


def launch(kernel, scalars, others, grid, in_specs, out_specs, out_shape, scratch_shapes=(), **options):
    skip = len(others)

    def run(*refs):
        kernel(*refs[:scalars], *refs[scalars + skip :])

    call = pl.pallas_call(
        run,
        out_shape=out_shape,
        grid_spec=pltpu.PrefetchScalarGridSpec(
            num_scalar_prefetch=scalars,
            grid=grid,
            in_specs=[pl.BlockSpec(memory_space=pl.ANY)] * skip + list(in_specs),
            out_specs=out_specs,
            scratch_shapes=list(scratch_shapes),
        ),
        **options,
    )
    return lambda *operands: call(*operands[:scalars], *others, *operands[scalars:])


def params(steps, mib):
    return pltpu.CompilerParams(
        dimension_semantics=("arbitrary",) * steps, vmem_limit_bytes=mib * 2**20
    )


def prepare_kernel(order_ref, q_ref, k_ref, v_ref, scale_ref, gain_ref, cos_ref, sin_ref, qo, ko, vo):
    cosine, sine = cos_ref[...], sin_ref[...]
    for which, (source, target) in enumerate(((q_ref, qo), (k_ref, ko))):
        scale = scale_ref[:, which : which + 1]
        for start in range(0, source.shape[1], HEAD):
            at = slice(start, start + HEAD)
            part = source[:, at] * scale * gain_ref[which : which + 1, at]
            turned = part * cosine + pltpu.roll(part, HEAD // 2, 1) * sine
            target[:, at] = turned.astype(low_type)
    vo[...] = v_ref[...].astype(low_type)


def prepare(projected, scales, gains, cosine, sine, order, stream):
    length, width = projected.shape[0] // 2, projected.shape[1] // 3
    count = order.shape[0]
    block = length // count
    out = pl.BlockSpec((block, width), lambda b, o: (o[b], 0))
    turn = pl.BlockSpec((block, HEAD), lambda b, o: (o[b], 0))
    return pl.pallas_call(
        prepare_kernel,
        out_shape=(jax.ShapeDtypeStruct((length, width), low_type),) * 3,
        grid_spec=pltpu.PrefetchScalarGridSpec(
            num_scalar_prefetch=1,
            grid=(count,),
            in_specs=[
                pl.BlockSpec((block, width), lambda b, o: (2 * b + stream, 0)),
                pl.BlockSpec((block, width), lambda b, o: (2 * b + stream, 1)),
                pl.BlockSpec((block, width), lambda b, o: (2 * b + stream, 2)),
                pl.BlockSpec((block, 2), lambda b, o: (2 * b + stream, 0)),
                pl.BlockSpec((2, width), lambda b, o: (0, 0)),
                turn,
                turn,
            ],
            out_specs=(out, out, out),
        ),
        compiler_params=params(1, 32),
        cost_estimate=brief,
        name="prepare",
    )(order, projected, projected, projected, scales, gains, cosine, sine)


def restore_kernel(
    order_ref,
    dq_ref,
    dk_ref,
    dv_ref,
    q_ref,
    k_ref,
    scale_ref,
    gain_ref,
    cos_ref,
    sin_ref,
    out_ref,
    value_ref,
    dot_ref,
    sum_ref,
):
    cosine, sine = cos_ref[...] * score_scale, sin_ref[...] * score_scale
    width = q_ref.shape[1]

    @pl.when(pl.program_id(0) == 0)
    def _():
        sum_ref[...] = jnp.zeros_like(sum_ref)

    for which, (source, pre) in enumerate(((dq_ref, q_ref), (dk_ref, k_ref))):
        scale = scale_ref[:, which : which + 1]
        dots = 0.0
        for start in range(0, width, HEAD):
            at = slice(start, start + HEAD)
            part = source[:, at]
            turned = part * cosine - pltpu.roll(part, HEAD // 2, 1) * sine
            weighted = turned * gain_ref[which : which + 1, at]
            unit = pre[:, at] * scale
            out_ref[:, which * width + start : which * width + start + HEAD] = weighted
            dots = dots + jnp.sum(weighted * unit, axis=1, keepdims=True)
            sum_ref[which : which + 1, at] += jnp.sum(turned * unit, axis=0, keepdims=True)
        dot_ref[:, which : which + 1] = dots
    value_ref[...] = dv_ref[...].astype(low_type)


def restore(grads, projected, scales, gains, cosine, sine, order, stream):
    length, width = grads[0].shape
    count = order.shape[0]
    block = length // count
    first = stream * count
    later = pl.BlockSpec((block, width), lambda b, o: (first + o[b], 0))
    turn = pl.BlockSpec((block, HEAD), lambda b, o: (o[b], 0))
    both = pl.BlockSpec((block, 2), lambda b, o: (b, 0))
    scale = pl.BlockSpec((block, 2), lambda b, o: (2 * b + stream, 0))
    small = pl.BlockSpec((2, width), lambda b, o: (0, 0))
    return pl.pallas_call(
        restore_kernel,
        out_shape=(
            jax.ShapeDtypeStruct((length, 2 * width), jnp.float32),
            jax.ShapeDtypeStruct((length, width), low_type),
            jax.ShapeDtypeStruct((length, 2), jnp.float32),
            jax.ShapeDtypeStruct((2, width), jnp.float32),
        ),
        grid_spec=pltpu.PrefetchScalarGridSpec(
            num_scalar_prefetch=1,
            grid=(count,),
            in_specs=[
                pl.BlockSpec((block, width), lambda b, o: (o[b], 0)),
                later,
                later,
                pl.BlockSpec((block, width), lambda b, o: (2 * b + stream, 0)),
                pl.BlockSpec((block, width), lambda b, o: (2 * b + stream, 1)),
                scale,
                small,
                turn,
                turn,
            ],
            out_specs=(
                pl.BlockSpec((block, 2 * width), lambda b, o: (b, 0)),
                pl.BlockSpec((block, width), lambda b, o: (b, 0)),
                both,
                small,
            ),
        ),
        compiler_params=params(1, 40),
        cost_estimate=brief,
        name="restore",
    )(order, *grads, projected, projected, scales, gains, cosine, sine)


def finish_kernel(weighted_ref, q_ref, k_ref, scale_ref, mean_ref, value_ref, out_ref):
    width = q_ref.shape[1]
    for which, pre in enumerate((q_ref, k_ref)):
        at = slice(which * width, (which + 1) * width)
        scale = scale_ref[:, which : which + 1]
        unit = pre[...] * scale
        inward = scale * (weighted_ref[:, at] - unit * mean_ref[:, which : which + 1])
        out_ref[:, at] = inward.astype(low_type)
    out_ref[:, 2 * width :] = value_ref[...]


def finish(weighted, projected, scales, means, values, count, stream):
    length, width = values.shape
    block = length // count
    scale = pl.BlockSpec((block, 2), lambda b: (2 * b + stream, 0))
    return launch(
        finish_kernel,
        0,
        [],
        grid=(count,),
        out_shape=jax.ShapeDtypeStruct((length, 3 * width), low_type),
        in_specs=[
            pl.BlockSpec((block, 2 * width), lambda b: (b, 0)),
            pl.BlockSpec((block, width), lambda b: (2 * b + stream, 0)),
            pl.BlockSpec((block, width), lambda b: (2 * b + stream, 1)),
            scale,
            pl.BlockSpec((block, 2), lambda b: (b, 0)),
            pl.BlockSpec((block, width), lambda b: (b, 0)),
        ],
        out_specs=pl.BlockSpec((block, 3 * width), lambda b: (b, 0)),
        compiler_params=params(1, 40),
        cost_estimate=brief,
        name="finish",
    )(weighted, projected, projected, scales, means, values)


def causal(tile):
    key = lax.broadcasted_iota(jnp.int32, (tile, tile), 0)
    query = lax.broadcasted_iota(jnp.int32, (tile, tile), 1)
    return key <= query


def forward_kernel(tile, parts, spots_ref, q_ref, *refs):
    k_refs, v_refs = refs[:parts], refs[parts : 2 * parts]
    o_ref, log_ref, ks, vt, held_rows = refs[2 * parts :]
    rows = k_refs[0].shape[0]
    step = pl.program_id(1)

    @pl.when(step == 0)
    def _():
        for part in range(parts):
            ks[part * rows : (part + 1) * rows, :] = k_refs[part][...]
            for start in range(0, rows, tile):
                at = slice(part * rows + start, part * rows + start + tile)
                value = v_refs[part][start : start + tile, :]
                vt[:, at] = value.astype(jnp.float32).T.astype(low_type)

    query = q_ref[...]

    def visit(j, carry, masked):
        top, mass, held = carry
        at = pl.ds(pl.multiple_of(j * tile, tile), tile)
        scores = against(ks[at, :], query)
        if masked:
            scores = jnp.where(causal(tile), scores, masked_value)
        new_top = jnp.maximum(top, jnp.max(scores, axis=0, keepdims=True))
        weights = jnp.exp2((scores - new_top) * exponent_scale)
        fade = jnp.exp2((top - new_top) * exponent_scale)
        mass = mass * fade + jnp.sum(weights, axis=0, keepdims=True)
        held = held * fade + product(vt[:, at], weights.astype(low_type))
        return new_top, mass, held

    start = (
        jnp.full((1, tile), masked_value, jnp.float32),
        jnp.zeros((1, tile), jnp.float32),
        jnp.zeros((HEAD, tile), jnp.float32),
    )
    last = step + (parts - 1) * (rows // tile)
    carry = visit(last, start, True)
    top, mass, held = lax.fori_loop(0, last, lambda j, c: visit(j, c, False), carry)
    here = pl.ds(pl.multiple_of(step * tile, tile), tile)
    held_rows[here, :] = (held / mass).T.astype(low_type)
    log_ref[0] = top * exponent_scale + jnp.log2(mass)

    @pl.when(step == rows // tile - 1)
    def _():
        count = spots_ref.shape[0]
        block = rows // count
        for k in range(count):
            there = pl.ds(pl.multiple_of(spots_ref[k] * block, block), block)
            o_ref[k * block : (k + 1) * block, :] = held_rows[there, :]


def attend_forward(queries, keys, values, spots):
    (queries,), others = untie(queries)
    length, width = queries.shape
    heads, parts = width // HEAD, len(keys)
    tile = tile_of(length)
    whole = pl.BlockSpec((length, HEAD), lambda h, i, o: (0, h))
    piece = pl.BlockSpec((tile, HEAD), lambda h, i, o: (i, h))
    return launch(
        functools.partial(forward_kernel, tile, parts),
        1,
        others,
        out_shape=(
            jax.ShapeDtypeStruct((length, width), low_type),
            jax.ShapeDtypeStruct((heads, 1, length), jnp.float32),
        ),
        grid=(heads, length // tile),
        in_specs=[piece] + [whole] * (2 * parts),
        out_specs=(whole, pl.BlockSpec((1, 1, tile), lambda h, i, o: (h, 0, i))),
        scratch_shapes=[
            pltpu.VMEM((parts * length, HEAD), low_type),
            pltpu.VMEM((HEAD, parts * length), low_type),
            pltpu.VMEM((length, HEAD), low_type),
        ],
        compiler_params=params(2, 40),
        cost_estimate=brief,
        name="attend_forward",
    )(spots, queries, *keys, *values)


def backward_kernel(tile, parts, extra, spots_ref, q_ref, g_ref, o_ref, log_ref, *refs):
    k_refs, v_refs = refs[:parts], refs[parts : 2 * parts]
    added = refs[2 * parts : 2 * parts + extra]
    dq_ref, dk_ref, dv_ref, ks, vs, kt, gs, os, delta, dqt = refs[2 * parts + extra :]
    rows = q_ref.shape[0]
    steps = rows // tile
    step = pl.program_id(1)

    @pl.when(step == 0)
    def _():
        for part in range(parts):
            ks[part * rows : (part + 1) * rows, :] = k_refs[part][...]
            vs[part * rows : (part + 1) * rows, :] = v_refs[part][...]
            for start in range(0, rows, tile):
                at = slice(part * rows + start, part * rows + start + tile)
                key = k_refs[part][start : start + tile, :]
                kt[:, at] = key.astype(jnp.float32).T.astype(low_type)
        count = spots_ref.shape[0]
        block = rows // count
        for k in range(count):
            there = pl.ds(pl.multiple_of(spots_ref[k] * block, block), block)
            gs[there, :] = g_ref[k * block : (k + 1) * block, :]
            os[there, :] = o_ref[k * block : (k + 1) * block, :]
        for start in range(0, rows, tile):
            at = slice(start, start + tile)
            both = gs[at, :].astype(jnp.float32) * os[at, :].astype(jnp.float32)
            delta[:, at] = jnp.sum(both.T, axis=0, keepdims=True)
        dqt[...] = jnp.zeros_like(dqt)

    here = pl.ds(pl.multiple_of(step * tile, tile), tile)
    key, value, key_turned = ks[here, :], vs[here, :], kt[:, here]

    def visit(i, carry, masked):
        key_sum, value_sum = carry
        at = pl.ds(pl.multiple_of(i * tile, tile), tile)
        query, outward = q_ref[at, :], gs[at, :]
        scores = against(key, query)
        exact = jnp.exp2(scores * exponent_scale - log_ref[0, :, at])
        if masked:
            exact = jnp.where(causal(tile), exact, 0.0)
        slope = (exact * (against(value, outward) - delta[:, at])).astype(low_type)
        value_sum = value_sum + product(exact.astype(low_type), outward)
        key_sum = key_sum + product(slope, query)
        dqt[:, at] += product(key_turned, slope)
        return key_sum, value_sum

    if extra:
        carry = (added[0][...], added[1][...])
    else:
        carry = (jnp.zeros((tile, HEAD), jnp.float32),) * 2
    own = step - (parts - 1) * steps

    def store(carry):
        dk_ref[...], dv_ref[...] = carry

    @pl.when(own < 0)
    def _():
        store(lax.fori_loop(0, steps, lambda i, c: visit(i, c, False), carry))

    @pl.when(own >= 0)
    def _():
        first = visit(own, carry, True)
        store(lax.fori_loop(own + 1, steps, lambda i, c: visit(i, c, False), first))

    @pl.when(own == steps - 1)
    def _():
        for start in range(0, rows, tile):
            at = slice(start, start + tile)
            dq_ref[at, :] = dqt[:, at].T


def attend_backward(queries, outward, attended, logs, keys, values, added, spots):
    (queries,), others = untie(queries)
    length, width = queries.shape
    heads, parts = width // HEAD, len(keys)
    tile = tile_of(length)
    whole = pl.BlockSpec((length, HEAD), lambda h, j, o: (0, h))
    piece = pl.BlockSpec((tile, HEAD), lambda h, j, o: (j, h))
    total = parts * length
    return launch(
        functools.partial(backward_kernel, tile, parts, len(added)),
        1,
        others,
        out_shape=(
            jax.ShapeDtypeStruct((length, width), jnp.float32),
            jax.ShapeDtypeStruct((total, width), jnp.float32),
            jax.ShapeDtypeStruct((total, width), jnp.float32),
        ),
        grid=(heads, total // tile),
        in_specs=[whole] * 3
        + [pl.BlockSpec((1, 1, length), lambda h, j, o: (h, 0, 0))]
        + [whole] * (2 * parts)
        + [piece] * len(added),
        out_specs=(whole, piece, piece),
        scratch_shapes=[
            pltpu.VMEM((total, HEAD), low_type),
            pltpu.VMEM((total, HEAD), low_type),
            pltpu.VMEM((HEAD, total), low_type),
            pltpu.VMEM((length, HEAD), low_type),
            pltpu.VMEM((length, HEAD), low_type),
            pltpu.VMEM((1, length), jnp.float32),
            pltpu.VMEM((HEAD, length), jnp.float32),
        ],
        compiler_params=params(2, 48),
        cost_estimate=brief,
        name="attend_backward",
    )(spots, queries, outward, attended, logs, *keys, *values, *added)


def out_kernel(others_ref, x_ref, w_ref, out_ref):
    @pl.when(pl.program_id(1) == 0)
    def _():
        out_ref[...] = jnp.zeros_like(out_ref)

    out_ref[...] += product(x_ref[0], w_ref[...])


def out_project(pieces, weight, spots):
    (pieces,), others = untie(pieces)
    count, rows, depth = pieces.shape
    width = weight.shape[1]
    across = min(1024, width)
    return launch(
        out_kernel,
        1,
        others,
        out_shape=jax.ShapeDtypeStruct((rows, width), jnp.float32),
        grid=(width // across, count),
        in_specs=[
            pl.BlockSpec((1, rows, depth), lambda n, k, o: (k, 0, 0)),
            pl.BlockSpec((depth, across), lambda n, k, o: (o[k], n)),
        ],
        out_specs=pl.BlockSpec((rows, across), lambda n, k, o: (0, n)),
        compiler_params=params(2, 32),
        cost_estimate=brief,
        name="out_project",
    )(spots, pieces, weight)


def weave_kernel(odd_ref, own_ref, other_ref, out_ref):
    odd = odd_ref[0]
    for high in range(own_ref.shape[0]):
        out_ref[0, 0, 2 * high + odd] = own_ref[high, 0, 0]
        out_ref[0, 0, 2 * high + 1 - odd] = other_ref[high, 0, 0]


def weave(own, other, odd):
    half, dps, ctxs, rows, width = own.shape
    piece = pl.BlockSpec((half, 1, 1, rows, width), lambda i, j, o: (0, i, j, 0, 0))
    return pl.pallas_call(
        weave_kernel,
        out_shape=jax.ShapeDtypeStruct((dps, ctxs, 2 * half, rows, width), own.dtype),
        grid_spec=pltpu.PrefetchScalarGridSpec(
            num_scalar_prefetch=1,
            grid=(dps, ctxs),
            in_specs=[piece, piece],
            out_specs=pl.BlockSpec(
                (1, 1, 2 * half, rows, width), lambda i, j, o: (i, j, 0, 0, 0)
            ),
        ),
        compiler_params=params(2, 32),
        cost_estimate=brief,
        name="weave",
    )(odd, own, other)


def out_back_kernel(others_ref, x_ref, w_ref, out_ref):
    out_ref[0] = against(x_ref[...], w_ref[...]).astype(low_type)


def out_back(grad, weight, spots):
    (grad,), others = untie(grad)
    rows, width = grad.shape
    count = spots.shape[0]
    depth = weight.shape[0] // count
    return launch(
        out_back_kernel,
        1,
        others,
        out_shape=jax.ShapeDtypeStruct((count, rows, depth), low_type),
        grid=(count,),
        in_specs=[
            pl.BlockSpec((rows, width), lambda k, o: (0, 0)),
            pl.BlockSpec((depth, width), lambda k, o: (o[k], 0)),
        ],
        out_specs=pl.BlockSpec((1, rows, depth), lambda k, o: (k, 0, 0)),
        compiler_params=params(1, 32),
        cost_estimate=brief,
        name="out_back",
    )(spots, grad, weight)


def out_weight_kernel(streams, others_ref, *refs):
    lefts, rights, out_ref = refs[:streams], refs[streams:-1], refs[-1]
    total = 0.0
    for left, right in zip(lefts, rights):
        total = total + product(left[0].T, right[...])
    out_ref[...] = total.astype(low_type)


def out_weight(lefts, rights, spots):
    lefts, others = untie(*lefts)
    count, rows, depth = lefts[0].shape
    width = rights[0].shape[1]
    across = min(1024, width)
    return launch(
        functools.partial(out_weight_kernel, len(lefts)),
        1,
        others,
        out_shape=jax.ShapeDtypeStruct((count * depth, width), low_type),
        grid=(width // across, count),
        in_specs=[pl.BlockSpec((1, rows, depth), lambda n, k, o: (k, 0, 0))] * len(lefts)
        + [pl.BlockSpec((rows, across), lambda n, k, o: (0, n))] * len(rights),
        out_specs=pl.BlockSpec((depth, across), lambda n, k, o: (o[k], n)),
        compiler_params=params(2, 32),
        cost_estimate=brief,
        name="out_weight",
    )(spots, *lefts, *rights)


def chosen(refs, index, use):
    for i, ref in enumerate(refs):
        pl.when(index == i)(functools.partial(use, ref))


def gate_up_kernel(count, parts, *refs):
    pieces, refs = refs[:count], refs[count:]
    gates, ups = refs[:parts], refs[parts : 2 * parts]
    gate_ref, up_ref, inner_ref = refs[2 * parts :]
    half = pieces[0].shape[1] // parts

    def use(x_ref):
        gate = up = 0.0
        for p in range(parts):
            piece = x_ref[:, p * half : (p + 1) * half]
            gate = gate + product(piece, gates[p][...])
            up = up + product(piece, ups[p][...])
        gate_ref[...] = gate.astype(low_type)
        up_ref[...] = up.astype(low_type)
        inner_ref[...] = (gate * jax.nn.sigmoid(gate) * up).astype(low_type)

    chosen(pieces, pl.program_id(1), use)


def gate_up(pieces, gates, ups):
    pieces, others = untie(*pieces)
    count, (rows, width) = len(pieces), pieces[0].shape
    parts, columns = len(gates), gates[0].shape[1]
    across = min(512, columns)
    weight = pl.BlockSpec((width // parts, across), lambda n, m: (0, n))
    out = pl.BlockSpec((rows, across), lambda n, m: (m, n))
    return launch(
        functools.partial(gate_up_kernel, count, parts),
        0,
        others,
        grid=(columns // across, count),
        out_shape=(jax.ShapeDtypeStruct((count * rows, columns), low_type),) * 3,
        in_specs=[pl.BlockSpec((rows, width), lambda n, m: (0, 0))] * count
        + [weight] * (2 * parts),
        out_specs=(out,) * 3,
        compiler_params=params(2, 52),
        cost_estimate=brief,
        name="gate_up",
    )(*pieces, *gates, *ups)


def spread_kernel(terms, parts, *refs):
    lefts, weights, out = refs[:terms], refs[terms:-1], refs[-1]
    for p in range(parts):
        total = 0.0
        for t in range(terms):
            total = total + against(lefts[t][...], weights[t * parts + p][...])
        out[p] = total.astype(low_type)


def spread(lefts, weights, half):
    lefts, others = untie(*lefts)
    rows, columns = lefts[0].shape[0] // 2, lefts[0].shape[1]
    terms, parts, features = len(lefts), len(weights[0]), weights[0][0].shape[0]
    across = min(256, features)
    return launch(
        functools.partial(spread_kernel, terms, parts),
        0,
        others,
        grid=(features // across,),
        out_shape=jax.ShapeDtypeStruct((parts, rows, features), low_type),
        in_specs=[pl.BlockSpec((rows, columns), lambda n: (half, 0))] * terms
        + [pl.BlockSpec((across, columns), lambda n: (n, 0))] * (terms * parts),
        out_specs=pl.BlockSpec((parts, rows, across), lambda n: (0, 0, n)),
        compiler_params=params(1, 52),
        cost_estimate=brief,
        name="spread",
    )(*lefts, *[w for group in weights for w in group])


def inner_kernel(count, parts, *refs):
    pieces, (gate_ref, up_ref), refs = refs[:count], refs[count : count + 2], refs[count + 2 :]
    weights, (dgate_ref, dup_ref) = refs[:parts], refs[parts:]
    half = pieces[0].shape[1] // parts

    def use(x_ref):
        grad = 0.0
        for p in range(parts):
            grad = grad + product(x_ref[:, p * half : (p + 1) * half], weights[p][...])
        gate, up = gate_ref[...].astype(jnp.float32), up_ref[...].astype(jnp.float32)
        sigma = jax.nn.sigmoid(gate)
        dgate_ref[...] = (grad * up * sigma * (1.0 + gate * (1.0 - sigma))).astype(low_type)
        dup_ref[...] = (grad * gate * sigma).astype(low_type)

    chosen(pieces, pl.program_id(1), use)


def inner_backward(pieces, gate, up, downs):
    (gate,), others = untie(gate)
    count, (rows, width) = len(pieces), pieces[0].shape
    parts, columns = len(downs), downs[0].shape[1]
    across = min(1024, columns)
    out = pl.BlockSpec((rows, across), lambda n, m: (m, n))
    return launch(
        functools.partial(inner_kernel, count, parts),
        0,
        others,
        grid=(columns // across, count),
        out_shape=(jax.ShapeDtypeStruct((count * rows, columns), low_type),) * 2,
        in_specs=[pl.BlockSpec((rows, width), lambda n, m: (0, 0))] * count
        + [out, out]
        + [pl.BlockSpec((width // parts, across), lambda n, m: (0, n))] * parts,
        out_specs=(out,) * 2,
        compiler_params=params(2, 52),
        cost_estimate=brief,
        name="inner_backward",
    )(*pieces, gate, up, *downs)


def weight_kernel(count, each, *refs):
    lefts, rights, (out, turned) = refs[:count], refs[count : count + count // each], refs[-2:]
    rows = lefts[0].shape[0]

    @pl.when(pl.program_id(1) == 0)
    def _():
        for c in range(count):
            turned[:, c * rows : (c + 1) * rows] = lefts[c][...].T

    total = 0.0
    for s, right in enumerate(rights):
        at = slice(s * each * rows, (s + 1) * each * rows)
        total = total + product(turned[:, at], right[...])
    out[...] = total.astype(low_type)


def weight_gradient(lefts, rights, start, size):
    lefts, others = [list(left) for left in lefts], untie(*[v for left in lefts for v in left])[1]
    lefts = [[plain(v) for v in left] for left in lefts]
    each, rows = len(lefts[0]), lefts[0][0].shape[0]
    columns, count = rights[0].shape[1], len(lefts) * each
    tile = min(512, size)
    across = next(a for a in (1024, 768, 512, 384, 128) if columns % a == 0)
    first = start // tile
    return launch(
        functools.partial(weight_kernel, count, each),
        0,
        others,
        grid=(size // tile, columns // across),
        out_shape=jax.ShapeDtypeStruct((size, columns), low_type),
        in_specs=[pl.BlockSpec((rows, tile), lambda m, n: (0, first + m))] * count
        + [pl.BlockSpec((each * rows, across), lambda m, n: (0, n))] * len(rights),
        out_specs=pl.BlockSpec((tile, across), lambda m, n: (m, n)),
        scratch_shapes=[pltpu.VMEM((tile, count * rows), low_type)],
        compiler_params=params(2, 52),
        cost_estimate=brief,
        name="weight_gradient",
    )(*[left for group in lefts for left in group], *rights)


def update_kernel(steps, columns_ref, *refs):
    grads, (w, m, v, g_out, m_out, v_out, w_out) = refs[: len(steps)], refs[len(steps) :]
    step = pl.program_id(0)
    first = 0
    for count, grad_ref in zip(steps, grads):

        @pl.when((step >= first) & (step < first + count))
        def _(grad_ref=grad_ref):
            gradient = grad_ref[...].astype(jnp.float32)
            moment, square, weight = adamw(
                w[...], m[...], v[...], gradient, learn_rate, weight_decay
            )
            g_out[...] = gradient
            m_out[...] = moment
            v_out[...] = square
            w_out[...] = weight

        first += count


def update(grads, columns, across, weight, moment, square):
    rows, width = weight.shape
    steps = [g.shape[0] // rows * (g.shape[1] // across) for g in grads]
    specs, first = [], 0
    for g, count in zip(grads, steps):
        per = g.shape[1] // across

        def place(i, c, first=first, count=count, per=per):
            at = jnp.clip(i - first, 0, count - 1)
            return at // per, at % per

        specs.append(pl.BlockSpec((rows, across), place))
        first += count
    here = pl.BlockSpec((rows, across), lambda i, c: (0, c[i]))
    return pl.pallas_call(
        functools.partial(update_kernel, steps),
        out_shape=(jax.ShapeDtypeStruct((rows, width), jnp.float32),) * 4,
        grid_spec=pltpu.PrefetchScalarGridSpec(
            num_scalar_prefetch=1,
            grid=(sum(steps),),
            in_specs=specs + [here] * 3,
            out_specs=(here,) * 4,
        ),
        compiler_params=params(1, 40),
        cost_estimate=brief,
        name="update",
    )(columns, *grads, weight, moment, square)


def swap(value, axis, bits):
    size = lax.axis_size(axis)
    return lax.ppermute(value, axis, [(i, i ^ bits) for i in range(size)])


def pick(pieces, index):
    return lax.dynamic_index_in_dim(pieces, index, axis=0, keepdims=False)


def trade(pieces, axis):
    size, me = lax.axis_size(axis), lax.axis_index(axis)
    mine = pick(pieces, me)
    out = jnp.zeros((size,) + mine.shape, mine.dtype)
    out = lax.dynamic_update_index_in_dim(out, mine, me, 0)
    for bits in range(1, size):
        got = swap(pick(pieces, me ^ bits), axis, bits)
        out = lax.dynamic_update_index_in_dim(out, got, me ^ bits, 0)
    return out


def trade_near(pieces, axis):
    return [pieces[0]] + [swap(pieces[k], axis, k) for k in range(1, lax.axis_size(axis))]


def total_of(value, axes):
    for axis in axes:
        bits = 1
        while bits < lax.axis_size(axis):
            value = value + swap(value, axis, bits)
            bits *= 2
    return value


def gather_pairs(value, axis, stop=0):
    size, me = lax.axis_size(axis), lax.axis_index(axis)
    bits, value = size // 2, value[None]
    while bits > stop:
        other = swap(value, axis, bits)
        low = (me & bits) == 0
        value = jnp.stack([jnp.where(low, value, other), jnp.where(low, other, value)], axis=1)
        value = value.reshape((-1,) + value.shape[2:])
        bits //= 2
    return value


def sum_pairs(pieces, axis):
    size, me = lax.axis_size(axis), lax.axis_index(axis)
    bits = 1
    while bits < size:
        pieces = pieces.reshape((-1, 2) + pieces.shape[1:])
        mine = (me & bits) // bits
        keep = lax.dynamic_index_in_dim(pieces, mine, axis=1, keepdims=False)
        send = lax.dynamic_index_in_dim(pieces, 1 - mine, axis=1, keepdims=False)
        got = swap(send, axis, bits)
        pieces = (keep.astype(jnp.float32) + got.astype(jnp.float32)).astype(pieces.dtype)
        bits *= 2
    return pieces[0]


def near_order(size):
    return list(range(1, size, 2)) + list(range(0, size, 2))


def gather_group(value, axis):
    size = lax.axis_size(axis)
    got, bits = {0: value}, size // 2
    while bits:
        for known in sorted(got):
            got[known ^ bits] = swap(got[known], axis, bits)
        bits //= 2
    return [got[k] for k in near_order(size)]


def sum_group(got, kept, axis):
    size = lax.axis_size(axis)
    parts, bits, low = got.shape[0], 2, got.dtype
    shape = (parts, size // 2, -1) + got.shape[2:]
    pieces, got = kept.reshape(shape), got.reshape(shape)
    while bits < size:
        pieces = pieces.reshape((parts, -1, 2) + pieces.shape[2:])
        got = got.reshape(pieces.shape)
        send = pieces[:, :, 1].astype(jnp.float32) + got[:, :, 1].astype(jnp.float32)
        pieces = pieces[:, :, 0].astype(jnp.float32) + got[:, :, 0].astype(jnp.float32)
        got = swap(send.astype(low), axis, bits)
        bits *= 2
    return pieces[:, 0], got[:, 0]


def joined(terms):
    return list(terms[0].astype(jnp.float32) + terms[1].astype(jnp.float32))


def own_first(parts, axis):
    size, me = lax.axis_size(axis), lax.axis_index(axis)
    bits = 1
    while bits < size:
        parts = [jnp.where((me & bits) == 0, parts[i], parts[i ^ bits]) for i in range(size)]
        bits *= 2
    return jnp.concatenate(parts, axis=1)


def adamw(weight, moment, square, gradient, rate, decay):
    moment_new = beta_first * moment + (1.0 - beta_first) * gradient
    square_new = beta_second * square + (1.0 - beta_second) * gradient * gradient
    fix_first = 1.0 - beta_first**STEP
    fix_second = 1.0 - beta_second**STEP
    update = moment_new / fix_first / (jnp.sqrt(square_new / fix_second) + epsilon_adam)
    return (moment_new, square_new, weight - rate * (update + decay * weight))


def body(
    tokens,
    cotangent,
    pairing,
    attention_weights,
    attention_moment,
    attention_square,
    feed_weights,
    feed_moment,
    feed_square,
    gains,
    gain_moment,
    gain_square,
):
    inputs = tokens[0, 0]
    rows, width = inputs.shape
    dps, ctxs, groups = lax.axis_size("dp"), lax.axis_size("ctx"), lax.axis_size("fsdp")
    ctx = lax.axis_index("ctx")
    block = rows // 2
    length = block * ctxs
    owned = attention_weights.shape[0]
    hidden = feed_weights.shape[1] // 3
    part = hidden // groups
    head_width = width // ctxs
    upstream = cotangent[0, 0].astype(jnp.float32)

    rows_of = (slice(0, block), slice(block, rows))
    orders = (pairing[0, 0], ctxs - 1 - pairing[0, 0])
    turns = [turn_tables(start + jnp.arange(length, dtype=jnp.int32)) for start in (0, length)]

    def own_rows(own):
        return lax.all_gather(own, "ctx", axis=0, tiled=True)

    def both_rows(own):
        return [own] + [swap(own, "dp", bits) for bits in range(1, dps)]

    hold = lax.optimization_barrier
    inputs_all = lax.all_gather(inputs, "ctx", axis=0, tiled=True)
    qkv_low = attention_weights[:, : 3 * width].astype(low_type)
    qkv_low = qkv_low.reshape(owned, 3, ctxs, head_width).transpose(2, 0, 1, 3)
    qkv_low = qkv_low.reshape(ctxs, owned, 3 * head_width)
    feed_low = feed_weights.astype(low_type)
    qkv_low = trade(qkv_low, "ctx")
    feed_low = feed_low.reshape(owned, 3, groups, part).transpose(2, 1, 0, 3)
    feed_low = trade(feed_low, "fsdp").transpose(1, 0, 2, 3).reshape(3, groups * owned, part)
    qkv_low = gather_pairs(gather_pairs(qkv_low, "dp"), "fsdp")
    qkv_low = qkv_low.transpose(1, 2, 0, 3, 4).reshape(width, 3 * head_width)
    out_low = attention_weights[:, 3 * width :].astype(low_type)
    out_low = gather_pairs(gather_pairs(out_low, "ctx"), "dp")
    inputs_all, qkv_low, feed_low, out_low, turns = lax.optimization_barrier(
        (inputs_all, qkv_low, feed_low, out_low, turns)
    )

    near = jnp.arange(ctxs, dtype=jnp.int32) ^ ctx
    spots = [jnp.sum(jnp.where(near[:, None] == jnp.arange(ctxs), o, 0), axis=1) for o in orders]
    qk_gains = jnp.stack(
        [lax.dynamic_slice_in_dim(gains[i], ctx * head_width, head_width) for i in range(2)]
    )
    queries, keys, values = [], [], []
    attended, logs, attended_near = [], [], []
    projs, proj_scales, states, chunks = [], [], [], []
    projected = product(inputs_all, qkv_low)
    feed_own = [feed_low[0], feed_low[1], feed_low[2]]
    feed_own[0] = own_rows(feed_own[0])
    projected, feed_own[0], feed_own[1] = hold((projected, feed_own[0], feed_own[1]))
    gates = both_rows(feed_own[0])
    pre = [projected[:, i * head_width : (i + 1) * head_width] for i in range(2)]
    squares = total_of(jnp.stack([jnp.sum(p * p, axis=-1) for p in pre]), ("ctx",))
    scales = lax.rsqrt(squares / width + epsilon_norm).T
    for s in range(2):
        q, k, v = prepare(projected, scales, qk_gains, *turns[s], orders[s], s)
        queries.append(q)
        keys.append(k)
        values.append(v)

    def attend(s, last):
        out, log = attend_forward(after(queries[s], last), keys[: s + 1], values[: s + 1], spots[s])
        attended.append(out)
        logs.append(log)
        return trade_near(out.reshape(ctxs, block, head_width), "ctx")

    def leave(s, pieces, *others):
        attended_near.append(jnp.stack(pieces))
        proj = out_project(after(attended_near[s], *others), out_low, near)
        projs.append(proj)
        proj_scales.append(
            lax.rsqrt(jnp.mean(proj * proj, axis=-1, keepdims=True) + epsilon_norm)
        )
        states.append(
            inputs[rows_of[s]].astype(jnp.float32) + proj * proj_scales[s] * gains[2]
        )
        state_low = states[s].astype(low_type)
        state_low = own_first(jnp.split(state_low, dps, axis=1), "dp")
        chunks.append(gather_group(state_low, "fsdp"))

    out_low, scales = hold((out_low, scales))
    out_low = gather_pairs(out_low, "fsdp", 1)
    feed_own[1] = own_rows(feed_own[1])
    lower = attend(0, gates[0])
    out_low, feed_own[1], feed_own[2], attended[0] = hold(
        (out_low, feed_own[1], feed_own[2], attended[0])
    )
    out_other = swap(out_low, "fsdp", 1)
    ups = both_rows(feed_own[1])
    feed_own[2] = own_rows(feed_own[2])
    upper = attend(1, after(ups[0], gates[-1]))
    out_other, lower, upper, attended[1] = hold((out_other, lower, upper, attended[1]))
    odd = (lax.axis_index("fsdp") & 1)[None]
    out_low = weave(out_low, out_other, odd).reshape(width, width)
    leave(0, lower, gates[-1], ups[-1])
    leave(1, upper, states[0])
    feed_own[2], states[0] = hold((feed_own[2], states[0]))
    downs = both_rows(feed_own[2])

    gate, up, inner = [None] * 2, [None] * 2, [None] * 2
    outs, grad_downs, gain_downs = [None] * 2, [None] * 2, [None] * 2
    last, sums = downs[0], [None] * 2
    for s in range(2):
        chunks[s][-1] = after(chunks[s][-1], last)
        gate[s], up[s], inner[s] = gate_up(chunks[s], gates, ups)
        last = inner[s]
    for s in range(2):
        last = spread([after(inner[s], last)], [downs], 0)
        got = swap(last, "fsdp", 1)
        last = spread([after(inner[s], last)], [downs], 1)
        sums[s] = sum_group(got, last, "fsdp")
        last = after(last, got)
    grad_gates, grad_ups, grad_states = [None] * 2, [None] * 2, [None] * 2
    for s in range(2):
        if s == 1:
            grad_gates[0], grad_ups[0] = inner_backward(grad_downs[0], gate[0], up[0], downs)
            sums[1], grad_ups[0] = hold((sums[1], grad_ups[0]))
        down = own_first(joined(sums[s]), "dp")
        down_scale = lax.rsqrt(jnp.mean(down * down, axis=-1, keepdims=True) + epsilon_norm)
        outs[s] = (states[s] + down * down_scale * gains[3]).astype(low_type)
        grad_down, gain_downs[s] = norm_backward(
            down, down_scale, gains[3], upstream[rows_of[s]]
        )
        grad_down = own_first(jnp.split(grad_down.astype(low_type), dps, axis=1), "dp")
        grad_downs[s] = gather_group(grad_down, "fsdp")
    output_states = jnp.concatenate(outs, axis=0)

    grad_projs, grad_heads, gain_branches = [None] * 2, [None] * 2, [None] * 2
    size = width // dps

    def inward(s, last):
        if grad_gates[s] is None:
            grad_gates[s], grad_ups[s] = inner_backward(
                grad_downs[s], after(gate[s], last), up[s], downs
            )
        last = grad_ups[s]
        last = spread([after(grad_gates[s], last), grad_ups[s]], [gates, ups], 0)
        got = swap(last, "fsdp", 1)
        last = spread([after(grad_gates[s], last), grad_ups[s]], [gates, ups], 1)
        return sum_group(got, last, "fsdp"), after(last, got)

    def gradient_parts(lefts, rights, which, last):
        lefts = [[after(left[0], last)] + left[1:] for left in lefts]
        found = [weight_gradient(lefts, rights, bits * size, size) for bits in which]
        return found, found[-1]

    def outward(s, sums):
        grad_states[s] = upstream[rows_of[s]] + own_first(joined(sums), "dp")
        grad_proj, gain_branches[s] = norm_backward(
            projs[s], proj_scales[s], gains[2], grad_states[s]
        )
        grad_projs[s] = grad_proj.astype(low_type)
        grad_attended = out_back(grad_projs[s], out_low, near)
        grad_heads[s] = trade_near(grad_attended, "ctx")
        return grad_attended

    away, own = range(1, dps), range(1)
    def kept_feed(own, others):
        kept = own[0].astype(jnp.float32)
        for other in others:
            kept = kept + other.astype(jnp.float32)
        return kept.astype(low_type)

    def reduce_feed(kept):
        return lax.psum_scatter(kept, "ctx", scatter_dimension=0, tiled=True)

    def exchanged(pieces):
        return [swap(piece, "dp", bits) for bits, piece in zip(away, pieces)]

    away, own = range(1, dps), range(1)
    lower_sums, last = inward(0, downs[-1])
    down_away, last = gradient_parts(grad_downs, inner, away, last)
    down_away = exchanged(down_away)
    upper_sums, last = inward(1, last)
    gate_away, last = gradient_parts(chunks, grad_gates, away, last)
    upper_sums, gate_away = hold((upper_sums, gate_away))
    gate_away = exchanged(gate_away)
    last = outward(1, upper_sums)
    down_near, last = gradient_parts(grad_downs, inner, own, last)
    down_kept = kept_feed(down_near, down_away)
    lower_sums, down_kept, grad_heads[1] = hold((lower_sums, down_kept, grad_heads[1]))
    down_gradient = reduce_feed(down_kept)
    last = outward(0, lower_sums)
    up_away, last = gradient_parts(chunks, grad_ups, away, last)
    up_away = exchanged(up_away)
    gate_near, last = gradient_parts(chunks, grad_gates, own, last)
    up_near, last = gradient_parts(chunks, grad_ups, own, after(last, *grad_heads[1]))
    up_near, gate_away = hold((up_near, gate_away))
    gate_kept = kept_feed(gate_near, gate_away)
    gate_gradient = reduce_feed(gate_kept)
    queries[1] = after(queries[1], last, gate_kept)

    fsdp = lax.axis_index("fsdp")

    def feed_trade(piece):
        piece = piece.reshape(groups, owned, part)
        return trade_near([pick(piece, fsdp ^ k) for k in range(groups)], "fsdp")

    def stream_rows(values, s):
        return values.reshape((ctxs, 2, block) + values.shape[1:])[:, s].reshape(
            (length,) + values.shape[1:]
        )

    added, grad_inputs, grad_projected = (), [None] * 2, [None] * 2
    gain_qk = 0.0
    for s in (1, 0):
        if s == 0:
            down_traded = feed_trade(down_gradient)
            added, grad_part, down_traded = hold((added, grad_part, down_traded))
            grad_inputs[1] = lax.psum_scatter(grad_part, "ctx", scatter_dimension=0, tiled=True)
        grads = attend_backward(
            queries[s],
            jnp.concatenate(grad_heads[s], axis=0),
            attended[s],
            logs[s],
            keys[: s + 1],
            values[: s + 1],
            added,
            spots[s],
        )
        if s == 1:
            grads, up_away, grad_heads[0] = hold((grads, up_away, grad_heads[0]))
            up_gradient = reduce_feed(kept_feed(up_near, up_away))
            attended_near[0] = after(attended_near[0], grads[0])
            out_gradient = out_weight(attended_near, grad_projs, near)
            out_gradient = out_gradient.reshape(dps, ctxs, groups, owned, width)
            out_gradient = sum_pairs(out_gradient.transpose(2, 0, 1, 3, 4), "fsdp")
        else:
            grads, out_gradient = hold((grads, out_gradient))
            out_gradient = sum_pairs(out_gradient, "dp")
        added = grads[1:]
        weighted, value_low, dots, gain_sums = restore(
            grads, projected, scales, qk_gains, *turns[s], orders[s], s
        )
        gain_qk = gain_qk + gain_sums
        means = total_of(dots.T, ("ctx",)).T / width
        grad_projected[s] = finish(
            weighted, projected, scales, means, value_low, ctxs, s
        )
        if s == 0:
            gate_gradient, up_gradient, grad_projected[0] = hold(
                (gate_gradient, up_gradient, grad_projected[0])
            )
            gate_traded = feed_trade(gate_gradient)
            up_traded = feed_trade(up_gradient)
            qkv_gradient = weight_gradient(
                [[stream_rows(inputs_all, 0)], [stream_rows(inputs_all, 1)]],
                grad_projected,
                0,
                width,
            )
            grad_projected[0], qkv_gradient = hold((grad_projected[0], qkv_gradient))
        grad_part = against(grad_projected[s], qkv_low).astype(low_type)
    grad_inputs[0] = lax.psum_scatter(grad_part, "ctx", scatter_dimension=0, tiled=True)
    out_gradient = sum_pairs(out_gradient, "ctx")
    input_gradient = jnp.concatenate(
        [grad_states[s] + grad_inputs[s].astype(jnp.float32) for s in range(2)], axis=0
    ).astype(low_type)

    qkv_gradient = qkv_gradient.reshape(dps, ctxs, groups, owned, 3 * head_width)
    qkv_gradient = sum_pairs(sum_pairs(qkv_gradient.transpose(2, 0, 1, 3, 4), "fsdp"), "dp")
    qkv_gradient = jnp.concatenate(
        trade_near([pick(qkv_gradient, ctx ^ k) for k in range(ctxs)], "ctx"), axis=0
    )

    feed_pieces = gate_traded + up_traded + list(down_traded)
    near_columns = jnp.arange(groups, dtype=jnp.int32) ^ fsdp
    feed_columns_of = jnp.concatenate([kind * groups + near_columns for kind in range(3)])
    feed_gradient, feed_moment_new, feed_square_new, feed_weights_new = update(
        [jnp.concatenate(feed_pieces, axis=0)],
        feed_columns_of,
        part,
        feed_weights,
        feed_moment,
        feed_square,
    )
    attention_columns = jnp.concatenate(
        [
            (jnp.arange(3, dtype=jnp.int32)[None, :] * ctxs + near[:, None]).reshape(-1),
            3 * ctxs + jnp.arange(ctxs, dtype=jnp.int32),
        ]
    )
    attention_gradient, attention_moment_new, attention_square_new, attention_weights_new = update(
        [qkv_gradient, out_gradient],
        attention_columns,
        head_width,
        attention_weights,
        attention_moment,
        attention_square,
    )

    wide = lax.dynamic_update_slice(
        jnp.zeros((2, width), jnp.float32), gain_qk, (0, ctx * head_width)
    )
    gain_gradient = total_of(
        jnp.concatenate([wide, jnp.stack([sum(gain_branches), sum(gain_downs)])], axis=0), EVERY
    )
    gain_moment_new, gain_square_new, gains_new = adamw(
        gains, gain_moment, gain_square, gain_gradient, gain_rate, 0.0
    )
    return (
        output_states[None, None],
        input_gradient[None, None],
        attention_gradient,
        attention_moment_new,
        attention_square_new,
        attention_weights_new,
        feed_gradient,
        feed_moment_new,
        feed_square_new,
        feed_weights_new,
        gain_gradient,
        gain_moment_new,
        gain_square_new,
        gains_new,
    )


def solution(mesh):
    token = P("dp", "fsdp", "ctx", None)
    row = P(EVERY, None)
    return jax.shard_map(
        body,
        mesh=mesh,
        in_specs=(token, token, P("dp", "fsdp", None)) + (row,) * 6 + (P(),) * 3,
        out_specs=(token, token) + (row,) * 8 + (P(),) * 4,
        check_vma=False,
    )
```
